32 devices in a mesh: tensor: 4 (over y, x), context: 8 (over z, core).
Axes of the slice: x: 2, y: 2, z: 4, core: 2. Of those that a mesh axis runs over, the one named last changes fastest.
Arguments:
- query_gate: bfloat16 [1024, 4096], P('context', 'tensor'), may hold values from -6 to 6
- key_gate: bfloat16 [1024, 4096], P('context', 'tensor'), may hold values from -6 to 6
- value_in: bfloat16 [1024, 4096], P('context', 'tensor'), may hold values from -6 to 6
- filter_raw: float32 [1024, 256], P('context', 'tensor'), may hold values from -6 to 6
- grad_out: bfloat16 [1024, 4096], P('context', 'tensor'), may hold values from -6 to 6
Outputs:
- output: bfloat16 [1024, 4096], P('context', 'tensor')
- grad_query: bfloat16 [1024, 4096], P('context', 'tensor')
- grad_key: bfloat16 [1024, 4096], P('context', 'tensor')
- grad_value: bfloat16 [1024, 4096], P('context', 'tensor')
- grad_filter: float32 [1024, 256], P('context', 'tensor')
The draws below stay inside these ranges and needn't reach their ends.
All inputs are finite; a program needn't handle non-finite values.
Results may differ from the reference program's by a relative error of at most 0.0011.
Values sent between devices are 32-bit elements; how exact they have to be, the bound alone decides.
A program may use at most 64 MiB of HBM per device.

```python
import math
import jax
import jax.numpy as jnp
from jax import lax

CH_DEV = 1024
GROUP = 16
SEQ = 1024
CHANNELS = 4096
FILT_DEV = 64
FILTERS = 256
N_TENSOR = 4


def block_scale(stream_key, shape, shards, least, largest):
    factor_of, own = 1.0, jax.random.fold_in(stream_key, 6)
    for position, blocks in shards:
        steps = jnp.exp(jax.random.uniform(jax.random.fold_in(own, position), (blocks,), jnp.float32, least / len(shards), largest / len(shards)))
        factor_of = factor_of * jnp.repeat(steps, shape[position] // blocks).reshape([-1 if axis == position else 1 for axis in range(len(shape))])
    return factor_of


def centred(key, shape, deviation, reach, split=(), held_as=jnp.bfloat16):
    loudness = block_scale(key, shape, split, -0.22, 0.18) if split else 1.0
    result = jax.random.normal(key, shape, jnp.float32) * deviation * loudness
    return jnp.minimum(jnp.maximum(result, -reach), reach).astype(held_as)


def setup_inputs(seed: int = 0) -> dict:
    splits = jax.random.split(jax.random.key(seed), 6)
    return {
        "query_gate": centred(splits[0], (SEQ, CHANNELS), 1.0, 6.0, ((0, 8), (1, 4))),
        "key_gate": centred(splits[1], (SEQ, CHANNELS), 1.0, 6.0, ((0, 8), (1, 4))),
        "value_in": centred(splits[2], (SEQ, CHANNELS), 1.0, 6.0, ((0, 8), (1, 4))),
        "filter_raw": centred(splits[3], (SEQ, FILTERS), 1.0, 6.0, ((0, 8), (1, 4)), jnp.float32),
        "grad_out": centred(splits[4], (SEQ, CHANNELS), 1.0, 6.0, ((0, 8), (1, 4))),
    }


def one_slab(pieces):
    query_gate, key_gate, value_in, filter_raw, grad_out = pieces
    points = 2 * SEQ
    scale = 1.0 / math.sqrt(SEQ)
    query_full = query_gate.astype(jnp.float32)
    key_full = key_gate.astype(jnp.float32)
    value_full = value_in.astype(jnp.float32)
    grad_full = grad_out.astype(jnp.float32)
    gated = key_full * value_full
    filt = jnp.repeat(filter_raw.astype(jnp.float32) * scale, GROUP, axis=1)
    spec_gated = jnp.fft.rfft(gated, n=points, axis=0)
    spec_filt = jnp.fft.rfft(filt, n=points, axis=0)
    grad_conv = grad_full * query_full
    spec_grad = jnp.fft.rfft(grad_conv, n=points, axis=0)
    conv = jnp.fft.irfft(spec_gated * spec_filt, n=points, axis=0)[:SEQ]
    grad_gated = jnp.fft.irfft(jnp.conj(spec_filt) * spec_grad, n=points, axis=0)[:SEQ]
    corr = jnp.fft.irfft(jnp.conj(spec_gated) * spec_grad, n=points, axis=0)[:SEQ]
    output = (query_full * conv).astype(jnp.bfloat16)
    grad_query = (grad_full * conv).astype(jnp.bfloat16)
    grad_key = (grad_gated * value_full).astype(jnp.bfloat16)
    grad_value = (grad_gated * key_full).astype(jnp.bfloat16)
    grad_filter = (lax.optimization_barrier(jnp.sum(corr.reshape(SEQ, FILT_DEV, GROUP), axis=2)) * scale).astype(jnp.float32)
    return (output, grad_query, grad_key, grad_value, grad_filter)

def split_slabs(array, count):
    return jnp.transpose(array.reshape(SEQ, N_TENSOR, count), (1, 0, 2))

def join_slabs(array):
    return jnp.transpose(array, (1, 0, 2)).reshape(SEQ, -1)

def reference(query_gate, key_gate, value_in, filter_raw, grad_out):
    pieces = (split_slabs(query_gate, CH_DEV), split_slabs(key_gate, CH_DEV), split_slabs(value_in, CH_DEV), split_slabs(filter_raw, FILT_DEV), split_slabs(grad_out, CH_DEV))
    results = lax.map(one_slab, pieces)
    return (join_slabs(results[0]), join_slabs(results[1]), join_slabs(results[2]), join_slabs(results[3]), join_slabs(results[4]))
```

```python
import functools
import math

import jax
import jax.numpy as jnp
import numpy as np
from jax import lax
from jax.experimental import pallas as pl
from jax.experimental.pallas import tpu as pltpu
from jax.sharding import PartitionSpec as P

highest = lax.Precision.HIGHEST


def phase_table(count_rows, count_cols, period):
    row_index = lax.broadcasted_iota(jnp.int32, (count_rows, count_cols), 0)
    col_index = lax.broadcasted_iota(jnp.int32, (count_rows, count_cols), 1)
    return (row_index * col_index % period).astype(jnp.float32) * (2.0 * math.pi / period)


def rotate(real_part, imag_part, cosine, sine):
    return (real_part * cosine - imag_part * sine, real_part * sine + imag_part * cosine)


def local(query_gate, key_gate, value_in, filter_raw, grad_out):
    groups = lax.axis_size("context")
    here = lax.axis_index("context")
    rows = query_gate.shape[0]
    width = query_gate.shape[1]
    filter_count = filter_raw.shape[1]
    group_size = width // filter_count
    points = 2 * groups * rows
    scale = 1.0 / math.sqrt(groups * rows)
    local_phase = phase_table(rows, rows, rows)
    cos_local = jnp.cos(local_phase)
    sin_local = jnp.sin(local_phase)
    row_iota = lax.broadcasted_iota(jnp.int32, (1, rows, 1), 1)
    parity = lax.broadcasted_iota(jnp.int32, (2, 1, 1), 0)

    def twiddle_phase(first):
        frequency = 2 * first + parity
        return (row_iota * frequency % points).astype(jnp.float32) * (2.0 * math.pi / points)

    def transpose_forward(signal):
        pieces = lax.all_to_all(signal[None], "context", split_axis=1, concat_axis=0, tiled=True)
        angles = phase_table(2 * groups, groups, 2 * groups)
        spread_re = jnp.einsum("ap,plc->alc", jnp.cos(angles), pieces, precision=highest)
        spread_im = -jnp.einsum("ap,plc->alc", jnp.sin(angles), pieces, precision=highest)
        return lax.all_to_all(
            jnp.stack([spread_re, spread_im]), "context", split_axis=1, concat_axis=2, tiled=True
        )

    def forward(signal):
        spec = transpose_forward(signal)
        phase = twiddle_phase(here)
        tw_re, tw_im = rotate(spec[0], spec[1], jnp.cos(phase), -jnp.sin(phase))
        out_re = jnp.einsum("br,erc->ebc", cos_local, tw_re, precision=highest) + jnp.einsum(
            "br,erc->ebc", sin_local, tw_im, precision=highest
        )
        out_im = jnp.einsum("br,erc->ebc", cos_local, tw_im, precision=highest) - jnp.einsum(
            "br,erc->ebc", sin_local, tw_re, precision=highest
        )
        return jnp.stack([out_re, out_im])

    def transpose_inverse(spec):
        pieces = lax.all_to_all(spec, "context", split_axis=2, concat_axis=1, tiled=True)
        angles = phase_table(groups, 2 * groups, 2 * groups)
        values = jnp.einsum(
            "pa,alc->plc", jnp.cos(angles), pieces[0], precision=highest
        ) - jnp.einsum("pa,alc->plc", jnp.sin(angles), pieces[1], precision=highest)
        return lax.all_to_all(values, "context", split_axis=0, concat_axis=1, tiled=True)[0]

    def turned(spec, first):
        loc_re = jnp.einsum("rb,ebc->erc", cos_local, spec[0], precision=highest) - jnp.einsum(
            "rb,ebc->erc", sin_local, spec[1], precision=highest
        )
        loc_im = jnp.einsum("rb,ebc->erc", cos_local, spec[1], precision=highest) + jnp.einsum(
            "rb,ebc->erc", sin_local, spec[0], precision=highest
        )
        phase = twiddle_phase(first)
        rot_re, rot_im = rotate(loc_re, loc_im, jnp.cos(phase), jnp.sin(phase))
        return jnp.stack([rot_re, rot_im])

    def inverse(spec):
        signal = transpose_inverse(turned(spec, here))
        return signal * (1.0 / points)

    def widen(part):
        spread = jnp.broadcast_to(part[..., None], part.shape + (group_size,))
        return spread.reshape(part.shape[:-1] + (width,))

    def group_total(part):
        return jnp.sum(part.reshape(part.shape[:-1] + (filter_count, group_size)), axis=-1)

    query_full = query_gate.astype(jnp.float32)
    key_full = key_gate.astype(jnp.float32)
    value_full = value_in.astype(jnp.float32)
    grad_full = grad_out.astype(jnp.float32)
    gated = key_full * value_full
    grad_conv = grad_full * query_full
    filt_part = filter_raw * scale
    spec_gated = forward(gated)
    spec_grad = forward(grad_conv)
    spec_filt = forward(filt_part)
    gated_re, gated_im = (spec_gated[0], spec_gated[1])
    filt_re, filt_im = (widen(spec_filt[0]), widen(spec_filt[1]))
    grad_re, grad_im = (spec_grad[0], spec_grad[1])
    conv_spec = jnp.stack(
        [gated_re * filt_re - gated_im * filt_im, gated_re * filt_im + gated_im * filt_re]
    )
    back_spec = jnp.stack(
        [filt_re * grad_re + filt_im * grad_im, filt_re * grad_im - filt_im * grad_re]
    )
    corr_spec = jnp.stack(
        [
            group_total(gated_re * grad_re + gated_im * grad_im),
            group_total(gated_re * grad_im - gated_im * grad_re),
        ]
    )
    conv = inverse(conv_spec)
    grad_gated = inverse(back_spec)
    corr = inverse(corr_spec)
    output = (query_full * conv).astype(jnp.bfloat16)
    grad_query = (grad_full * conv).astype(jnp.bfloat16)
    grad_key = (grad_gated * value_full).astype(jnp.bfloat16)
    grad_value = (grad_gated * key_full).astype(jnp.bfloat16)
    grad_filter = corr * scale
    return (output, grad_query, grad_key, grad_value, grad_filter)


LANES = 128
VMEM_BUDGET = 40 * 2**20


def halves(table):
    high = jnp.asarray(table, jnp.float32).astype(jnp.bfloat16)
    low = (jnp.asarray(table, jnp.float32) - high.astype(jnp.float32)).astype(jnp.bfloat16)
    return high, low


def np_halves(table):
    table = table.astype(np.float32)
    high = table.astype(jnp.bfloat16)
    low = (table - high.astype(np.float32)).astype(jnp.bfloat16)
    return high, low


def tables(block):
    k = np.arange(block, dtype=np.float64)[:, None] + 0.5
    n = np.arange(-block, block, dtype=np.float64)[None, :]
    angle = (np.pi / block) * k * n
    return np.concatenate([np.cos(angle), -np.sin(angle)], axis=0)


NN = (((1,), (0,)), ((), ()))
NT = (((1,), (1,)), ((), ()))


def dot(a, b, dims=NN):
    return lax.dot_general(a, b, dims, preferred_element_type=jnp.float32)


def dot3(a, b, dims=NN):
    return dot(a[0], b[0], dims) + dot(a[0], b[1], dims) + dot(a[1], b[0], dims)


def kernel(chips, q_ref, k_ref, v_ref, go_ref, filt_ref, fwd_hi, fwd_lo, inv_hi, inv_lo, spread_ref,
           conv_ref, gg_ref, gf_ref,
           g_buf, r_buf, sg_buf, h_buf, h_spec, conv_acc, gg_acc, r_spec, c_spec, y_buf, x_buf, c_own, c_buf, f_buf,
           f_send, f_recv, e_send, e_recv, g_send, g_recv, r_send, r_recv, y_send, y_recv, c_send, c_recv, p_send, p_recv):
    groups = 2 * chips
    rows = q_ref.shape[0]
    half = q_ref.shape[1] // 2
    block = 2 * rows
    chunks = half // LANES
    nf = filt_ref.shape[0] // 2
    me = lax.axis_index("context")
    z, c = me // 2, me % 2
    partner = z * 2 + (1 - c)
    right = (me + 2) % groups
    left = (me + groups - 2) % groups

    def remote(src, dst, send, recv, target):
        return pltpu.make_async_remote_copy(
            src_ref=src, dst_ref=dst, send_sem=send, recv_sem=recv,
            device_id={"context": target}, device_id_type=pl.DeviceIdType.MESH)

    def columns(which, j):
        return pl.ds(pl.multiple_of(which * half + j * LANES, LANES), LANES)

    my_rows = pl.ds(pl.multiple_of(c * rows, rows), rows)
    its_rows = pl.ds(pl.multiple_of((1 - c) * rows, rows), rows)

    barrier = pltpu.get_barrier_semaphore()
    for d in range(1, groups):
        pl.semaphore_signal(barrier, inc=1, device_id={"context": (me + d) % groups},
                            device_id_type=pl.DeviceIdType.MESH)
    pl.semaphore_wait(barrier, groups - 1)

    def swap(which, j):
        buf = g_buf if which == 0 else r_buf
        return remote(sg_buf.at[which, j], buf.at[0, j, my_rows, :],
                      e_send.at[which, j], e_recv.at[which, j], partner)

    def gate_out(j, carry):
        cols = columns(1 - c, j)
        sg_buf[0, j] = k_ref[:, cols].astype(jnp.float32) * v_ref[:, cols].astype(jnp.float32)
        swap(0, j).start()
        sg_buf[1, j] = go_ref[:, cols].astype(jnp.float32) * q_ref[:, cols].astype(jnp.float32)
        swap(1, j).start()
        return carry

    lax.fori_loop(0, chunks, gate_out, 0)

    def filter_copy(d):
        target = (me + d) % groups
        part = pl.ds(pl.multiple_of((target % 2) * nf, nf), nf)
        return remote(filt_ref.at[part, :], h_buf.at[z, c], f_send.at[d], f_recv.at[d], target)

    for d in range(1, groups):
        filter_copy(d).start()
    h_buf[z, c] = filt_ref[pl.ds(pl.multiple_of(c * nf, nf), nf), :]

    def gate_own(j, carry):
        cols = columns(c, j)
        g_buf[0, j, my_rows, :] = k_ref[:, cols].astype(jnp.float32) * v_ref[:, cols].astype(jnp.float32)
        r_buf[0, j, my_rows, :] = go_ref[:, cols].astype(jnp.float32) * q_ref[:, cols].astype(jnp.float32)
        return carry

    lax.fori_loop(0, chunks, gate_own, 0)

    def g_copy(s, j):
        return remote(g_buf.at[s, j], g_buf.at[s + 1, j], g_send.at[s, j], g_recv.at[s, j], right)

    def r_copy(s, j):
        return remote(r_buf.at[s, j], r_buf.at[s + 1, j], r_send.at[s, j], r_recv.at[s, j], left)

    def first_sends(j, carry):
        swap(0, j).wait_recv()

        @pl.when(z + 1 < chips)
        def _():
            g_copy(0, j).start()

        swap(1, j).wait_recv()

        @pl.when(z >= 1)
        def _():
            r_copy(0, j).start()
        return carry

    lax.fori_loop(0, chunks, first_sends, 0)

    for d in range(1, groups):
        filter_copy(d).wait_recv()

    def lag_spectrum(m, carry):
        late = jnp.concatenate([h_buf[m, 0], h_buf[m, 1]], axis=1)
        before = jnp.maximum(m - 1, 0)
        early = jnp.concatenate([h_buf[before, 0], h_buf[before, 1]], axis=1)
        early = early * (m > 0).astype(jnp.float32)
        window = halves(jnp.concatenate([early, late], axis=1))
        spec = halves(dot3((fwd_hi[...], fwd_lo[...]), window, NT))

        def widen(j, inner):
            h_spec[m, j] = dot(spec[0], spread_ref[j]) + dot(spec[1], spread_ref[j])
            return inner

        lax.fori_loop(0, chunks, widen, 0)
        return carry

    lax.fori_loop(0, chips, lag_spectrum, 0)
    c_spec[...] = jnp.zeros_like(c_spec)

    def spectrum(signal):
        return dot3((fwd_hi[:, block:], fwd_lo[:, block:]), halves(signal))

    def conj_times(a, b):
        ar, ai, br, bi = a[:block], a[block:], b[:block], b[block:]
        return jnp.concatenate([ar * br + ai * bi, ar * bi - ai * br], axis=0)

    def times(a, b):
        ar, ai, br, bi = a[:block], a[block:], b[:block], b[block:]
        return jnp.concatenate([ar * br - ai * bi, ar * bi + ai * br], axis=0)

    def add_corr(m, j, g):
        prod = halves(conj_times(g, r_spec[j]))
        c_spec[m] += dot(spread_ref[j], prod[0], NT) + dot(spread_ref[j], prod[1], NT)

    def own_step(j, carry):
        r = spectrum(r_buf[0, j])
        r_spec[j] = r
        gg_acc[j] = conj_times(h_spec[0, j], r)
        g = spectrum(g_buf[0, j])
        conv_acc[j] = times(h_spec[0, j], g)
        add_corr(0, j, g)
        return carry

    lax.fori_loop(0, chunks, own_step, 0)

    def y_copy(which, j):
        return remote(y_buf.at[which, j, its_rows, :], x_buf.at[which, j],
                      y_send.at[which, j], y_recv.at[which, j], partner)

    def finish(j):
        for which, acc, out in ((0, conv_acc, conv_ref), (1, gg_acc, gg_ref)):
            y_buf[which, j] = dot3((inv_hi[...], inv_lo[...]), halves(acc[j]))
            y_copy(which, j).start()
            out[:, columns(c, j)] = y_buf[which, j, my_rows, :]

    for s in range(chips - 1):
        def step(j, carry):
            @pl.when(z - 1 - s >= 0)
            def _():
                g_copy(s, j).wait_recv()
                if s < chips - 2:
                    @pl.when(z + 1 < chips)
                    def _():
                        g_copy(s + 1, j).start()
                g = spectrum(g_buf[s + 1, j])
                conv_acc[j] += times(h_spec[s + 1, j], g)
                add_corr(s + 1, j, g)

            @pl.when(z + 1 + s < chips)
            def _():
                r_copy(s, j).wait_recv()
                if s < chips - 2:
                    @pl.when(z >= 1)
                    def _():
                        r_copy(s + 1, j).start()
                gg_acc[j] += conj_times(h_spec[s + 1, j], spectrum(r_buf[s + 1, j]))

            if s == chips - 2:
                finish(j)
            return carry

        lax.fori_loop(0, chunks, step, 0)

    def lag_block(n):
        here = dot3(halves(c_spec[n]), (fwd_hi[:, block:], fwd_lo[:, block:]))
        after = dot3(halves(c_spec[n + 1]), (fwd_hi[:, :block], fwd_lo[:, :block]))
        return (here + after) * (1.0 / block)

    def c_copy(n):
        return remote(c_own.at[n], c_buf.at[z], c_send.at[n], c_recv.at[z], n * 2 + c)

    for n in range(chips):
        @pl.when(n <= z)
        def _():
            total = lag_block(n)
            c_own[n, 0] = total[:, :rows]
            c_own[n, 1] = total[:, rows:]

        @pl.when(n < z)
        def _():
            c_copy(n).start()

    for i in range(1, chips):
        @pl.when(i > z)
        def _():
            remote(c_own.at[0], c_buf.at[i], c_send.at[0], c_recv.at[i], partner).wait_recv()
            c_own[z] += c_buf[i]

    last = remote(c_own.at[z, 1 - c], f_buf, p_send, p_recv, partner)
    last.start()
    gf_ref[pl.ds(pl.multiple_of(c * nf, nf), nf), :] = c_own[z, c]

    def place(j, carry):
        for which, out in ((0, conv_ref), (1, gg_ref)):
            y_copy(which, j).wait_recv()
            out[:, columns(1 - c, j)] = x_buf[which, j]
        return carry

    lax.fori_loop(0, chunks, place, 0)
    last.wait_recv()
    gf_ref[pl.ds(pl.multiple_of((1 - c) * nf, nf), nf), :] = f_buf[...]

    last.wait_send()
    for n in range(chips - 1):
        @pl.when(n < z)
        def _():
            c_copy(n).wait_send()
    for d in range(1, groups):
        filter_copy(d).wait_send()

    def drain(j, carry):
        for which in range(2):
            swap(which, j).wait_send()
            y_copy(which, j).wait_send()
        for s in range(chips - 1):
            @pl.when((z - s >= 0) & (z + 1 < chips))
            def _():
                g_copy(s, j).wait_send()

            @pl.when((z + s < chips) & (z >= 1))
            def _():
                r_copy(s, j).wait_send()
        return carry

    lax.fori_loop(0, chunks, drain, 0)


def scratch(chips, rows, half, nf):
    chunks, block = half // LANES, 2 * rows
    f32 = jnp.float32
    memory = [
        (chips, chunks, block, LANES),
        (chips, chunks, block, LANES),
        (2, chunks, rows, LANES),
        (chips, 2, nf, rows),
        (chips, chunks, 2 * block, LANES),
        (chunks, 2 * block, LANES),
        (chunks, 2 * block, LANES),
        (chunks, 2 * block, LANES),
        (chips + 1, nf, 2 * block),
        (2, chunks, block, LANES),
        (2, chunks, rows, LANES),
        (chips, 2, nf, rows),
        (chips, 2, nf, rows),
        (nf, rows),
    ]
    steps = max(chips - 1, 1)
    sems = [
        (2 * chips,), (2 * chips,), (2, chunks), (2, chunks), (steps, chunks), (steps, chunks),
        (steps, chunks), (steps, chunks), (2, chunks), (2, chunks), (chips,), (chips,),
    ]
    used = sum(4 * math.prod(shape) for shape in memory)
    specs = [pltpu.VMEM(shape, f32) for shape in memory]
    specs += [pltpu.SemaphoreType.DMA(shape) for shape in sems]
    specs += [pltpu.SemaphoreType.DMA, pltpu.SemaphoreType.DMA]
    return used, specs


def fits(chips, rows, width, filters):
    used, _ = scratch(chips, rows, width // 2, filters // 2)
    aligned = rows % LANES == 0 and width % (2 * LANES) == 0 and filters % 16 == 0
    return aligned and chips >= 2 and used <= VMEM_BUDGET // 2


def local_fast(query_gate, key_gate, value_in, filter_raw, grad_out):
    groups = lax.axis_size("context")
    chips = groups // 2
    rows, width = query_gate.shape
    filters = filter_raw.shape[1]
    half, nf, block = width // 2, filters // 2, 2 * rows
    chunks = half // LANES
    scale = 1.0 / math.sqrt(groups * rows)
    forward = tables(block)
    fwd = np_halves(forward)
    inv = np_halves(forward[:, block:].T / block)
    spread = np.kron(np.eye(nf), np.ones((1, width // filters)))
    spread = spread.reshape(nf, chunks, LANES).transpose(1, 0, 2).astype(jnp.bfloat16)
    _, scratches = scratch(chips, rows, half, nf)
    vmem = pl.BlockSpec(memory_space=pltpu.VMEM)
    conv, grad_gated, corr = pl.pallas_call(
        functools.partial(kernel, chips),
        out_shape=(
            jax.ShapeDtypeStruct((rows, width), jnp.float32),
            jax.ShapeDtypeStruct((rows, width), jnp.float32),
            jax.ShapeDtypeStruct((filters, rows), jnp.float32),
        ),
        in_specs=[vmem] * 10,
        out_specs=(vmem,) * 3,
        scratch_shapes=scratches,
        compiler_params=pltpu.CompilerParams(
            collective_id=0, has_side_effects=True, vmem_limit_bytes=VMEM_BUDGET),
        cost_estimate=pl.CostEstimate(flops=10**10, bytes_accessed=8 * 2**20, transcendentals=0),
        name="ring_conv",
    )(query_gate, key_gate, value_in, grad_out, (filter_raw * scale).T, *fwd, *inv, spread)
    output = (query_gate.astype(jnp.float32) * conv).astype(jnp.bfloat16)
    grad_query = (grad_out.astype(jnp.float32) * conv).astype(jnp.bfloat16)
    grad_key = (grad_gated * value_in.astype(jnp.float32)).astype(jnp.bfloat16)
    grad_value = (grad_gated * key_gate.astype(jnp.float32)).astype(jnp.bfloat16)
    return output, grad_query, grad_key, grad_value, corr.T * scale


def dispatch(query_gate, key_gate, value_in, filter_raw, grad_out):
    args = (query_gate, key_gate, value_in, filter_raw, grad_out)
    rows, width = query_gate.shape
    if fits(lax.axis_size("context") // 2, rows, width, filter_raw.shape[1]):
        return local_fast(*args)
    return local(*args)


def solution(mesh):
    return jax.shard_map(
        dispatch,
        mesh=mesh,
        in_specs=(
            P("context", "tensor"),
            P("context", "tensor"),
            P("context", "tensor"),
            P("context", "tensor"),
            P("context", "tensor"),
        ),
        out_specs=(
            P("context", "tensor"),
            P("context", "tensor"),
            P("context", "tensor"),
            P("context", "tensor"),
            P("context", "tensor"),
        ),
        check_vma=False,
    )
```

```python
import functools
import math

import jax
import jax.numpy as jnp
import numpy as np
from jax import lax
from jax.experimental import pallas as pl
from jax.experimental.pallas import tpu as pltpu
from jax.sharding import PartitionSpec as P

highest = lax.Precision.HIGHEST


def phase_table(count_rows, count_cols, period):
    row_index = lax.broadcasted_iota(jnp.int32, (count_rows, count_cols), 0)
    col_index = lax.broadcasted_iota(jnp.int32, (count_rows, count_cols), 1)
    return (row_index * col_index % period).astype(jnp.float32) * (2.0 * math.pi / period)


def rotate(real_part, imag_part, cosine, sine):
    return (real_part * cosine - imag_part * sine, real_part * sine + imag_part * cosine)


def local(query_gate, key_gate, value_in, filter_raw, grad_out):
    groups = lax.axis_size("context")
    here = lax.axis_index("context")
    rows = query_gate.shape[0]
    width = query_gate.shape[1]
    filter_count = filter_raw.shape[1]
    group_size = width // filter_count
    points = 2 * groups * rows
    scale = 1.0 / math.sqrt(groups * rows)
    local_phase = phase_table(rows, rows, rows)
    cos_local = jnp.cos(local_phase)
    sin_local = jnp.sin(local_phase)
    row_iota = lax.broadcasted_iota(jnp.int32, (1, rows, 1), 1)
    parity = lax.broadcasted_iota(jnp.int32, (2, 1, 1), 0)

    def twiddle_phase(first):
        frequency = 2 * first + parity
        return (row_iota * frequency % points).astype(jnp.float32) * (2.0 * math.pi / points)

    def transpose_forward(signal):
        pieces = lax.all_to_all(signal[None], "context", split_axis=1, concat_axis=0, tiled=True)
        angles = phase_table(2 * groups, groups, 2 * groups)
        spread_re = jnp.einsum("ap,plc->alc", jnp.cos(angles), pieces, precision=highest)
        spread_im = -jnp.einsum("ap,plc->alc", jnp.sin(angles), pieces, precision=highest)
        return lax.all_to_all(
            jnp.stack([spread_re, spread_im]), "context", split_axis=1, concat_axis=2, tiled=True
        )

    def forward(signal):
        spec = transpose_forward(signal)
        phase = twiddle_phase(here)
        tw_re, tw_im = rotate(spec[0], spec[1], jnp.cos(phase), -jnp.sin(phase))
        out_re = jnp.einsum("br,erc->ebc", cos_local, tw_re, precision=highest) + jnp.einsum(
            "br,erc->ebc", sin_local, tw_im, precision=highest
        )
        out_im = jnp.einsum("br,erc->ebc", cos_local, tw_im, precision=highest) - jnp.einsum(
            "br,erc->ebc", sin_local, tw_re, precision=highest
        )
        return jnp.stack([out_re, out_im])

    def transpose_inverse(spec):
        pieces = lax.all_to_all(spec, "context", split_axis=2, concat_axis=1, tiled=True)
        angles = phase_table(groups, 2 * groups, 2 * groups)
        values = jnp.einsum(
            "pa,alc->plc", jnp.cos(angles), pieces[0], precision=highest
        ) - jnp.einsum("pa,alc->plc", jnp.sin(angles), pieces[1], precision=highest)
        return lax.all_to_all(values, "context", split_axis=0, concat_axis=1, tiled=True)[0]

    def turned(spec, first):
        loc_re = jnp.einsum("rb,ebc->erc", cos_local, spec[0], precision=highest) - jnp.einsum(
            "rb,ebc->erc", sin_local, spec[1], precision=highest
        )
        loc_im = jnp.einsum("rb,ebc->erc", cos_local, spec[1], precision=highest) + jnp.einsum(
            "rb,ebc->erc", sin_local, spec[0], precision=highest
        )
        phase = twiddle_phase(first)
        rot_re, rot_im = rotate(loc_re, loc_im, jnp.cos(phase), jnp.sin(phase))
        return jnp.stack([rot_re, rot_im])

    def inverse(spec):
        signal = transpose_inverse(turned(spec, here))
        return signal * (1.0 / points)

    def widen(part):
        spread = jnp.broadcast_to(part[..., None], part.shape + (group_size,))
        return spread.reshape(part.shape[:-1] + (width,))

    def group_total(part):
        return jnp.sum(part.reshape(part.shape[:-1] + (filter_count, group_size)), axis=-1)

    query_full = query_gate.astype(jnp.float32)
    key_full = key_gate.astype(jnp.float32)
    value_full = value_in.astype(jnp.float32)
    grad_full = grad_out.astype(jnp.float32)
    gated = key_full * value_full
    grad_conv = grad_full * query_full
    filt_part = filter_raw * scale
    spec_gated = forward(gated)
    spec_grad = forward(grad_conv)
    spec_filt = forward(filt_part)
    gated_re, gated_im = (spec_gated[0], spec_gated[1])
    filt_re, filt_im = (widen(spec_filt[0]), widen(spec_filt[1]))
    grad_re, grad_im = (spec_grad[0], spec_grad[1])
    conv_spec = jnp.stack(
        [gated_re * filt_re - gated_im * filt_im, gated_re * filt_im + gated_im * filt_re]
    )
    back_spec = jnp.stack(
        [filt_re * grad_re + filt_im * grad_im, filt_re * grad_im - filt_im * grad_re]
    )
    corr_spec = jnp.stack(
        [
            group_total(gated_re * grad_re + gated_im * grad_im),
            group_total(gated_re * grad_im - gated_im * grad_re),
        ]
    )
    conv = inverse(conv_spec)
    grad_gated = inverse(back_spec)
    corr = inverse(corr_spec)
    output = (query_full * conv).astype(jnp.bfloat16)
    grad_query = (grad_full * conv).astype(jnp.bfloat16)
    grad_key = (grad_gated * value_full).astype(jnp.bfloat16)
    grad_value = (grad_gated * key_full).astype(jnp.bfloat16)
    grad_filter = corr * scale
    return (output, grad_query, grad_key, grad_value, grad_filter)


LANES = 128
VMEM_BUDGET = 40 * 2**20


def halves(table):
    high = jnp.asarray(table, jnp.float32).astype(jnp.bfloat16)
    low = (jnp.asarray(table, jnp.float32) - high.astype(jnp.float32)).astype(jnp.bfloat16)
    return high, low


def np_halves(table):
    table = table.astype(np.float32)
    high = table.astype(jnp.bfloat16)
    low = (table - high.astype(np.float32)).astype(jnp.bfloat16)
    return high, low


def tables(block):
    k = np.arange(block, dtype=np.float64)[:, None] + 0.5
    n = np.arange(-block, block, dtype=np.float64)[None, :]
    angle = (np.pi / block) * k * n
    return np.concatenate([np.cos(angle), -np.sin(angle)], axis=0)


NN = (((1,), (0,)), ((), ()))
NT = (((1,), (1,)), ((), ()))


def dot(a, b, dims=NN):
    return lax.dot_general(a, b, dims, preferred_element_type=jnp.float32)


def dot3(a, b, dims=NN):
    return dot(a[0], b[0], dims) + dot(a[0], b[1], dims) + dot(a[1], b[0], dims)


def kernel(chips, q_hbm, k_hbm, v_hbm, go_hbm, filt_hbm, fwd_hi_hbm, fwd_lo_hbm, inv_hi_hbm, inv_lo_hbm, spread_hbm,
           conv_ref, gg_ref, gf_ref,
           q_ref, k_ref, v_ref, go_ref, filt_ref, fwd_hi, fwd_lo, inv_hi, inv_lo, spread_ref,
           g_buf, r_buf, sg_buf, h_buf, h_spec, conv_acc, gg_acc, r_spec, r_next, part_acc, part_buf, c_spec, y_buf, x_buf, c_own, c_buf, f_buf,
           f_send, f_recv, e_send, e_recv, g_send, g_recv, r_send, r_recv, y_send, y_recv, c_send, c_recv, load_sem, p_send, p_recv):
    groups = 2 * chips
    rows = q_ref.shape[0]
    half = q_ref.shape[1] // 2
    block = 2 * rows
    chunks = half // LANES
    nf = filt_ref.shape[0] // 2
    me = lax.axis_index("context")
    z, c = me // 2, me % 2
    partner = z * 2 + (1 - c)
    right = (me + 2) % groups
    left = (me + groups - 2) % groups

    def remote(src, dst, send, recv, target):
        return pltpu.make_async_remote_copy(
            src_ref=src, dst_ref=dst, send_sem=send, recv_sem=recv,
            device_id={"context": target}, device_id_type=pl.DeviceIdType.MESH)

    def columns(which, j):
        return pl.ds(pl.multiple_of(which * half + j * LANES, LANES), LANES)

    my_rows = pl.ds(pl.multiple_of(c * rows, rows), rows)
    its_rows = pl.ds(pl.multiple_of((1 - c) * rows, rows), rows)

    loads = [pltpu.make_async_copy(src, dst, load_sem.at[i]) for i, (src, dst) in enumerate((
        (k_hbm, k_ref), (v_hbm, v_ref), (go_hbm, go_ref), (q_hbm, q_ref), (filt_hbm, filt_ref),
        (fwd_hi_hbm, fwd_hi), (fwd_lo_hbm, fwd_lo), (spread_hbm, spread_ref), (inv_hi_hbm, inv_hi),
        (inv_lo_hbm, inv_lo)))]
    for load in loads:
        load.start()

    barrier = pltpu.get_barrier_semaphore()
    for d in range(1, groups):
        pl.semaphore_signal(barrier, inc=1, device_id={"context": (me + d) % groups},
                            device_id_type=pl.DeviceIdType.MESH)
    pl.semaphore_wait(barrier, groups - 1)
    for load in loads[:5]:
        load.wait()

    def swap(which, j):
        buf = g_buf if which == 0 else r_buf
        return remote(sg_buf.at[which, j], buf.at[0, j, my_rows, :],
                      e_send.at[which, j], e_recv.at[which, j], partner)

    def gate_out(j, carry):
        cols = columns(1 - c, j)
        sg_buf[0, j] = k_ref[:, cols].astype(jnp.float32) * v_ref[:, cols].astype(jnp.float32)
        swap(0, j).start()
        sg_buf[1, j] = go_ref[:, cols].astype(jnp.float32) * q_ref[:, cols].astype(jnp.float32)
        swap(1, j).start()
        return carry

    lax.fori_loop(0, chunks, gate_out, 0)

    def filter_copy(d):
        target = (me + d) % groups
        part = pl.ds(pl.multiple_of((target % 2) * nf, nf), nf)
        return remote(filt_ref.at[part, :], h_buf.at[z, c], f_send.at[d], f_recv.at[d], target)

    for d in range(1, groups):
        filter_copy(d).start()
    h_buf[z, c] = filt_ref[pl.ds(pl.multiple_of(c * nf, nf), nf), :]

    def gate_own(j, carry):
        cols = columns(c, j)
        g_buf[0, j, my_rows, :] = k_ref[:, cols].astype(jnp.float32) * v_ref[:, cols].astype(jnp.float32)
        r_buf[0, j, my_rows, :] = go_ref[:, cols].astype(jnp.float32) * q_ref[:, cols].astype(jnp.float32)
        return carry

    lax.fori_loop(0, chunks, gate_own, 0)

    def g_copy(s, j):
        return remote(g_buf.at[s, j], g_buf.at[s + 1, j], g_send.at[s, j], g_recv.at[s, j], right)

    def r_copy(s, j):
        return remote(r_buf.at[s, j], r_buf.at[s + 1, j], r_send.at[s, j], r_recv.at[s, j], left)

    def first_sends(j, carry):
        swap(0, j).wait_recv()

        @pl.when(z + 1 < chips)
        def _():
            g_copy(0, j).start()

        swap(1, j).wait_recv()

        @pl.when(z >= 1)
        def _():
            r_copy(0, j).start()
        return carry

    lax.fori_loop(0, chunks, first_sends, 0)

    for load in loads[5:]:
        load.wait()
    for d in range(1, groups):
        filter_copy(d).wait_recv()

    def lag_spectrum(m, carry):
        late = jnp.concatenate([h_buf[m, 0], h_buf[m, 1]], axis=1)
        before = jnp.maximum(m - 1, 0)
        early = jnp.concatenate([h_buf[before, 0], h_buf[before, 1]], axis=1)
        early = early * (m > 0).astype(jnp.float32)
        window = halves(jnp.concatenate([early, late], axis=1))
        spec = halves(dot3((fwd_hi[...], fwd_lo[...]), window, NT))

        def widen(j, inner):
            h_spec[m, j] = dot(spec[0], spread_ref[j]) + dot(spec[1], spread_ref[j])
            return inner

        lax.fori_loop(0, chunks, widen, 0)
        return carry

    lax.fori_loop(0, chips, lag_spectrum, 0)
    c_spec[...] = jnp.zeros_like(c_spec)

    def spectrum(signal):
        return dot3((fwd_hi[:, block:], fwd_lo[:, block:]), halves(signal))

    def conj_times(a, b):
        ar, ai, br, bi = a[:block], a[block:], b[:block], b[block:]
        return jnp.concatenate([ar * br + ai * bi, ar * bi - ai * br], axis=0)

    def times(a, b):
        ar, ai, br, bi = a[:block], a[block:], b[:block], b[block:]
        return jnp.concatenate([ar * br - ai * bi, ar * bi + ai * br], axis=0)

    def add_corr(m, j, g, r):
        prod = halves(conj_times(g, r))
        c_spec[m] += dot(spread_ref[j], prod[0], NT) + dot(spread_ref[j], prod[1], NT)

    def own_step(j, carry):
        r = spectrum(r_buf[0, j])
        r_spec[j] = r
        gg_acc[j] = conj_times(h_spec[0, j], r)
        g = spectrum(g_buf[0, j])
        conv_acc[j] = times(h_spec[0, j], g)
        add_corr(0, j, g, r)
        return carry

    lax.fori_loop(0, chunks, own_step, 0)

    def y_copy(which, j):
        return remote(y_buf.at[which, j, its_rows, :], x_buf.at[which, j],
                      y_send.at[which, j], y_recv.at[which, j], partner)

    def inverse(spec):
        return dot3((inv_hi[...], inv_lo[...]), halves(spec))

    def part_copy(which, j):
        if which == 0:
            return remote(part_buf.at[0, j], g_buf.at[2, j], g_send.at[1, j], g_recv.at[1, j], right)
        return remote(part_buf.at[1, j], r_buf.at[2, j], r_send.at[1, j], r_recv.at[1, j], left)

    def finish(j):
        for which, near, end in ((0, chips - 2, chips - 1), (1, 1, 0)):
            @pl.when(z == near)
            def _():
                part_buf[which, j] = inverse(part_acc[which, j])
                part_copy(which, j).start()

        for which, acc, out, end in ((0, conv_acc, conv_ref, chips - 1), (1, gg_acc, gg_ref, 0)):
            y_buf[which, j] = inverse(acc[j])

            @pl.when(z == end)
            def _():
                part_copy(which, j).wait_recv()
                y_buf[which, j] += (g_buf if which == 0 else r_buf)[2, j]

            y_copy(which, j).start()
            out[:, columns(c, j)] = y_buf[which, j, my_rows, :]

    last_step = chips - 3
    for s in range(last_step + 1):
        def step(j, carry):
            @pl.when((z + 1 + s < chips) & ((z >= 1) | (s == 0)))
            def _():
                r_copy(s, j).wait_recv()
                if s < last_step:
                    @pl.when(z >= 2)
                    def _():
                        r_copy(s + 1, j).start()
                r = spectrum(r_buf[s + 1, j])
                gg_acc[j] += conj_times(h_spec[s + 1, j], r)
                if s == 0:
                    r_next[j] = r

                @pl.when(z == 1)
                def _():
                    term = conj_times(h_spec[s + 2, j], r)
                    part_acc[1, j] = term if s == 0 else part_acc[1, j] + term

            @pl.when((z - 1 - s >= 0) & ((z <= chips - 2) | (s == 0)))
            def _():
                g_copy(s, j).wait_recv()
                if s < last_step:
                    @pl.when(z <= chips - 3)
                    def _():
                        g_copy(s + 1, j).start()
                g = spectrum(g_buf[s + 1, j])
                conv_acc[j] += times(h_spec[s + 1, j], g)
                add_corr(s + 1, j, g, r_spec[j])

                @pl.when(z == chips - 2)
                def _():
                    term = times(h_spec[s + 2, j], g)
                    part_acc[0, j] = term if s == 0 else part_acc[0, j] + term
                    add_corr(s + 2, j, g, r_next[j])

            if s == last_step:
                finish(j)
            return carry

        lax.fori_loop(0, chunks, step, 0)

    def lag_block(n):
        here = dot3(halves(c_spec[n]), (fwd_hi[:, block:], fwd_lo[:, block:]))
        after = dot3(halves(c_spec[n + 1]), (fwd_hi[:, :block], fwd_lo[:, :block]))
        return (here + after) * (1.0 / block)

    def c_copy(n):
        return remote(c_own.at[n], c_buf.at[z], c_send.at[n], c_recv.at[z], n * 2 + c)

    my_reach = jnp.where(z == chips - 2, chips - 1, jnp.where(z == chips - 1, 1, z))

    def reach(chip):
        return {chips - 2: chips - 1, chips - 1: 1}.get(chip, chip)

    for n in range(chips):
        @pl.when((n <= my_reach) | (n == z))
        def _():
            total = lag_block(n)
            c_own[n, 0] = total[:, :rows]
            c_own[n, 1] = total[:, rows:]

        @pl.when((n <= my_reach) & (n != z))
        def _():
            c_copy(n).start()

    for i in range(1, chips):
        @pl.when((z <= reach(i)) & (i != z))
        def _():
            remote(c_own.at[0], c_buf.at[i], c_send.at[0], c_recv.at[i], partner).wait_recv()
            c_own[z] += c_buf[i]

    last = remote(c_own.at[z, 1 - c], f_buf, p_send, p_recv, partner)
    last.start()
    gf_ref[pl.ds(pl.multiple_of(c * nf, nf), nf), :] = c_own[z, c]

    def place(j, carry):
        for which, out in ((0, conv_ref), (1, gg_ref)):
            y_copy(which, j).wait_recv()
            out[:, columns(1 - c, j)] = x_buf[which, j]
        return carry

    lax.fori_loop(0, chunks, place, 0)
    last.wait_recv()
    gf_ref[pl.ds(pl.multiple_of((1 - c) * nf, nf), nf), :] = f_buf[...]

    last.wait_send()
    for n in range(chips):
        @pl.when((n <= my_reach) & (n != z))
        def _():
            c_copy(n).wait_send()
    for d in range(1, groups):
        filter_copy(d).wait_send()

    def drain(j, carry):
        for which in range(2):
            swap(which, j).wait_send()
            y_copy(which, j).wait_send()
        for s in range(last_step + 1):
            @pl.when((z - s >= 0) & (z + 1 < (chips if s == 0 else chips - 1)))
            def _():
                g_copy(s, j).wait_send()

            @pl.when((z + s < chips) & (z >= (1 if s == 0 else 2)))
            def _():
                r_copy(s, j).wait_send()

        for which, near in ((0, chips - 2), (1, 1)):
            @pl.when(z == near)
            def _():
                part_copy(which, j).wait_send()
        return carry

    lax.fori_loop(0, chunks, drain, 0)


def scratch(chips, rows, half, nf):
    chunks, block = half // LANES, 2 * rows
    f32 = jnp.float32
    memory = [
        (chips, chunks, block, LANES),
        (chips, chunks, block, LANES),
        (2, chunks, rows, LANES),
        (chips, 2, nf, rows),
        (chips, chunks, 2 * block, LANES),
        (chunks, 2 * block, LANES),
        (chunks, 2 * block, LANES),
        (chunks, 2 * block, LANES),
        (chunks, 2 * block, LANES),
        (2, chunks, 2 * block, LANES),
        (2, chunks, block, LANES),
        (chips + 1, nf, 2 * block),
        (2, chunks, block, LANES),
        (2, chunks, rows, LANES),
        (chips, 2, nf, rows),
        (chips, 2, nf, rows),
        (nf, rows),
    ]
    steps = max(chips - 1, 1)
    sems = [
        (2 * chips,), (2 * chips,), (2, chunks), (2, chunks), (steps, chunks), (steps, chunks),
        (steps, chunks), (steps, chunks), (2, chunks), (2, chunks), (chips,), (chips,),
        (10,),
    ]
    used = sum(4 * math.prod(shape) for shape in memory)
    held = [((rows, 2 * half), jnp.bfloat16)] * 4 + [((2 * nf, rows), f32)]
    held += [((2 * block, 2 * block), jnp.bfloat16)] * 2 + [((block, 2 * block), jnp.bfloat16)] * 2
    held += [((chunks, nf, LANES), jnp.bfloat16)]
    specs = [pltpu.VMEM(shape, kind) for shape, kind in held]
    specs += [pltpu.VMEM(shape, f32) for shape in memory]
    specs += [pltpu.SemaphoreType.DMA(shape) for shape in sems]
    specs += [pltpu.SemaphoreType.DMA, pltpu.SemaphoreType.DMA]
    return used, specs


def fits(chips, rows, width, filters):
    used, _ = scratch(chips, rows, width // 2, filters // 2)
    aligned = rows % LANES == 0 and width % (2 * LANES) == 0 and filters % 16 == 0
    return aligned and chips >= 3 and used <= VMEM_BUDGET // 2


def local_fast(query_gate, key_gate, value_in, filter_raw, grad_out):
    groups = lax.axis_size("context")
    chips = groups // 2
    rows, width = query_gate.shape
    filters = filter_raw.shape[1]
    half, nf, block = width // 2, filters // 2, 2 * rows
    chunks = half // LANES
    scale = 1.0 / math.sqrt(groups * rows)
    forward = tables(block)
    fwd = np_halves(forward)
    inv = np_halves(forward[:, block:].T / block)
    spread = np.kron(np.eye(nf), np.ones((1, width // filters)))
    spread = spread.reshape(nf, chunks, LANES).transpose(1, 0, 2).astype(jnp.bfloat16)
    _, scratches = scratch(chips, rows, half, nf)
    vmem = pl.BlockSpec(memory_space=pltpu.VMEM)
    conv, grad_gated, corr = pl.pallas_call(
        functools.partial(kernel, chips),
        out_shape=(
            jax.ShapeDtypeStruct((rows, width), jnp.float32),
            jax.ShapeDtypeStruct((rows, width), jnp.float32),
            jax.ShapeDtypeStruct((filters, rows), jnp.float32),
        ),
        in_specs=[pl.BlockSpec(memory_space=pltpu.HBM)] * 10,
        out_specs=(vmem,) * 3,
        scratch_shapes=scratches,
        compiler_params=pltpu.CompilerParams(
            collective_id=0, has_side_effects=True, vmem_limit_bytes=VMEM_BUDGET),
        cost_estimate=pl.CostEstimate(flops=10**10, bytes_accessed=8 * 2**20, transcendentals=0),
        name="ring_conv",
    )(query_gate, key_gate, value_in, grad_out, (filter_raw * scale).T, *fwd, *inv, spread)
    output = (query_gate.astype(jnp.float32) * conv).astype(jnp.bfloat16)
    grad_query = (grad_out.astype(jnp.float32) * conv).astype(jnp.bfloat16)
    grad_key = (grad_gated * value_in.astype(jnp.float32)).astype(jnp.bfloat16)
    grad_value = (grad_gated * key_gate.astype(jnp.float32)).astype(jnp.bfloat16)
    return output, grad_query, grad_key, grad_value, corr.T * scale


def dispatch(query_gate, key_gate, value_in, filter_raw, grad_out):
    args = (query_gate, key_gate, value_in, filter_raw, grad_out)
    rows, width = query_gate.shape
    if fits(lax.axis_size("context") // 2, rows, width, filter_raw.shape[1]):
        return local_fast(*args)
    return local(*args)


def solution(mesh):
    return jax.shard_map(
        dispatch,
        mesh=mesh,
        in_specs=(
            P("context", "tensor"),
            P("context", "tensor"),
            P("context", "tensor"),
            P("context", "tensor"),
            P("context", "tensor"),
        ),
        out_specs=(
            P("context", "tensor"),
            P("context", "tensor"),
            P("context", "tensor"),
            P("context", "tensor"),
            P("context", "tensor"),
        ),
        check_vma=False,
    )
```

```python
import functools
import math

import jax
import jax.numpy as jnp
import numpy as np
from jax import lax
from jax.experimental import pallas as pl
from jax.experimental.pallas import tpu as pltpu
from jax.sharding import PartitionSpec as P

highest = lax.Precision.HIGHEST


def phase_table(count_rows, count_cols, period):
    row_index = lax.broadcasted_iota(jnp.int32, (count_rows, count_cols), 0)
    col_index = lax.broadcasted_iota(jnp.int32, (count_rows, count_cols), 1)
    return (row_index * col_index % period).astype(jnp.float32) * (2.0 * math.pi / period)


def rotate(real_part, imag_part, cosine, sine):
    return (real_part * cosine - imag_part * sine, real_part * sine + imag_part * cosine)


def local(query_gate, key_gate, value_in, filter_raw, grad_out):
    groups = lax.axis_size("context")
    here = lax.axis_index("context")
    rows = query_gate.shape[0]
    width = query_gate.shape[1]
    filter_count = filter_raw.shape[1]
    group_size = width // filter_count
    points = 2 * groups * rows
    scale = 1.0 / math.sqrt(groups * rows)
    local_phase = phase_table(rows, rows, rows)
    cos_local = jnp.cos(local_phase)
    sin_local = jnp.sin(local_phase)
    row_iota = lax.broadcasted_iota(jnp.int32, (1, rows, 1), 1)
    parity = lax.broadcasted_iota(jnp.int32, (2, 1, 1), 0)

    def twiddle_phase(first):
        frequency = 2 * first + parity
        return (row_iota * frequency % points).astype(jnp.float32) * (2.0 * math.pi / points)

    def transpose_forward(signal):
        pieces = lax.all_to_all(signal[None], "context", split_axis=1, concat_axis=0, tiled=True)
        angles = phase_table(2 * groups, groups, 2 * groups)
        spread_re = jnp.einsum("ap,plc->alc", jnp.cos(angles), pieces, precision=highest)
        spread_im = -jnp.einsum("ap,plc->alc", jnp.sin(angles), pieces, precision=highest)
        return lax.all_to_all(
            jnp.stack([spread_re, spread_im]), "context", split_axis=1, concat_axis=2, tiled=True
        )

    def forward(signal):
        spec = transpose_forward(signal)
        phase = twiddle_phase(here)
        tw_re, tw_im = rotate(spec[0], spec[1], jnp.cos(phase), -jnp.sin(phase))
        out_re = jnp.einsum("br,erc->ebc", cos_local, tw_re, precision=highest) + jnp.einsum(
            "br,erc->ebc", sin_local, tw_im, precision=highest
        )
        out_im = jnp.einsum("br,erc->ebc", cos_local, tw_im, precision=highest) - jnp.einsum(
            "br,erc->ebc", sin_local, tw_re, precision=highest
        )
        return jnp.stack([out_re, out_im])

    def transpose_inverse(spec):
        pieces = lax.all_to_all(spec, "context", split_axis=2, concat_axis=1, tiled=True)
        angles = phase_table(groups, 2 * groups, 2 * groups)
        values = jnp.einsum(
            "pa,alc->plc", jnp.cos(angles), pieces[0], precision=highest
        ) - jnp.einsum("pa,alc->plc", jnp.sin(angles), pieces[1], precision=highest)
        return lax.all_to_all(values, "context", split_axis=0, concat_axis=1, tiled=True)[0]

    def turned(spec, first):
        loc_re = jnp.einsum("rb,ebc->erc", cos_local, spec[0], precision=highest) - jnp.einsum(
            "rb,ebc->erc", sin_local, spec[1], precision=highest
        )
        loc_im = jnp.einsum("rb,ebc->erc", cos_local, spec[1], precision=highest) + jnp.einsum(
            "rb,ebc->erc", sin_local, spec[0], precision=highest
        )
        phase = twiddle_phase(first)
        rot_re, rot_im = rotate(loc_re, loc_im, jnp.cos(phase), jnp.sin(phase))
        return jnp.stack([rot_re, rot_im])

    def inverse(spec):
        signal = transpose_inverse(turned(spec, here))
        return signal * (1.0 / points)

    def widen(part):
        spread = jnp.broadcast_to(part[..., None], part.shape + (group_size,))
        return spread.reshape(part.shape[:-1] + (width,))

    def group_total(part):
        return jnp.sum(part.reshape(part.shape[:-1] + (filter_count, group_size)), axis=-1)

    query_full = query_gate.astype(jnp.float32)
    key_full = key_gate.astype(jnp.float32)
    value_full = value_in.astype(jnp.float32)
    grad_full = grad_out.astype(jnp.float32)
    gated = key_full * value_full
    grad_conv = grad_full * query_full
    filt_part = filter_raw * scale
    spec_gated = forward(gated)
    spec_grad = forward(grad_conv)
    spec_filt = forward(filt_part)
    gated_re, gated_im = (spec_gated[0], spec_gated[1])
    filt_re, filt_im = (widen(spec_filt[0]), widen(spec_filt[1]))
    grad_re, grad_im = (spec_grad[0], spec_grad[1])
    conv_spec = jnp.stack(
        [gated_re * filt_re - gated_im * filt_im, gated_re * filt_im + gated_im * filt_re]
    )
    back_spec = jnp.stack(
        [filt_re * grad_re + filt_im * grad_im, filt_re * grad_im - filt_im * grad_re]
    )
    corr_spec = jnp.stack(
        [
            group_total(gated_re * grad_re + gated_im * grad_im),
            group_total(gated_re * grad_im - gated_im * grad_re),
        ]
    )
    conv = inverse(conv_spec)
    grad_gated = inverse(back_spec)
    corr = inverse(corr_spec)
    output = (query_full * conv).astype(jnp.bfloat16)
    grad_query = (grad_full * conv).astype(jnp.bfloat16)
    grad_key = (grad_gated * value_full).astype(jnp.bfloat16)
    grad_value = (grad_gated * key_full).astype(jnp.bfloat16)
    grad_filter = corr * scale
    return (output, grad_query, grad_key, grad_value, grad_filter)


LANES = 128
VMEM_BUDGET = 40 * 2**20
VMEM_LIMIT = 60 * 2**20


def halves(table):
    high = jnp.asarray(table, jnp.float32).astype(jnp.bfloat16)
    low = (jnp.asarray(table, jnp.float32) - high.astype(jnp.float32)).astype(jnp.bfloat16)
    return high, low


def np_halves(table):
    table = table.astype(np.float32)
    high = table.astype(jnp.bfloat16)
    low = (table - high.astype(np.float32)).astype(jnp.bfloat16)
    return high, low


def tables(block):
    k = np.arange(block, dtype=np.float64)[:, None] + 0.5
    n = np.arange(-block, block, dtype=np.float64)[None, :]
    angle = (np.pi / block) * k * n
    return np.concatenate([np.cos(angle), -np.sin(angle)], axis=0)


NN = (((1,), (0,)), ((), ()))
NT = (((1,), (1,)), ((), ()))
TN = (((0,), (0,)), ((), ()))


def dot(a, b, dims=NN):
    return lax.dot_general(a, b, dims, preferred_element_type=jnp.float32)


def dot3(a, b):
    count = b[0].shape[1]
    wide = dot(a[0], jnp.concatenate(b, axis=1))
    return wide[:, :count] + wide[:, count:] + dot(a[1], b[0])


def kernel(chips, q_hbm, k_hbm, v_hbm, go_hbm, filt_hbm, fwd_hi_hbm, fwd_lo_hbm, inv_hi_hbm, inv_lo_hbm, spread_hbm, gather_hbm,
           conv_ref, gg_ref, gf_ref,
           q_ref, k_ref, v_ref, go_ref, filt_ref, fwd_hi, fwd_lo, inv_hi, inv_lo, spread_ref, gather_ref,
           g_buf, r_buf, sg_buf, h_buf, h_spec, conv_acc, gg_acc, r_spec, r_next, part_acc, part_buf, c_spec, y_buf, x_buf, c_own, c_buf, f_buf,
           f_send, f_recv, e_send, e_recv, g_send, g_recv, r_send, r_recv, y_send, y_recv, c_send, c_recv, load_sem, p_send, p_recv):
    groups = 2 * chips
    rows = q_ref.shape[0]
    half = q_ref.shape[1] // 2
    block = 2 * rows
    chunks = half // LANES
    nf = filt_ref.shape[0] // 2
    me = lax.axis_index("context")
    z, c = me // 2, me % 2
    partner = z * 2 + (1 - c)
    right = (me + 2) % groups
    left = (me + groups - 2) % groups

    def remote(src, dst, send, recv, target):
        return pltpu.make_async_remote_copy(
            src_ref=src, dst_ref=dst, send_sem=send, recv_sem=recv,
            device_id={"context": target}, device_id_type=pl.DeviceIdType.MESH)

    def columns(which, j):
        return pl.ds(pl.multiple_of(which * half + j * LANES, LANES), LANES)

    my_rows = pl.ds(pl.multiple_of(c * rows, rows), rows)
    its_rows = pl.ds(pl.multiple_of((1 - c) * rows, rows), rows)

    loads = [pltpu.make_async_copy(src, dst, load_sem.at[i]) for i, (src, dst) in enumerate((
        (k_hbm, k_ref), (v_hbm, v_ref), (go_hbm, go_ref), (q_hbm, q_ref), (filt_hbm, filt_ref),
        (fwd_hi_hbm, fwd_hi), (fwd_lo_hbm, fwd_lo), (spread_hbm, spread_ref), (gather_hbm, gather_ref), (inv_hi_hbm, inv_hi),
        (inv_lo_hbm, inv_lo)))]
    for load in loads:
        load.start()

    barrier = pltpu.get_barrier_semaphore()
    for d in range(1, groups):
        pl.semaphore_signal(barrier, inc=1, device_id={"context": (me + d) % groups},
                            device_id_type=pl.DeviceIdType.MESH)
    pl.semaphore_wait(barrier, groups - 1)
    for load in loads[:5]:
        load.wait()

    def swap(which, j):
        buf = g_buf if which == 0 else r_buf
        return remote(sg_buf.at[which, j], buf.at[0, j, my_rows, :],
                      e_send.at[which, j], e_recv.at[which, j], partner)

    def gate_out(j, carry):
        cols = columns(1 - c, j)
        sg_buf[0, j] = k_ref[:, cols].astype(jnp.float32) * v_ref[:, cols].astype(jnp.float32)
        swap(0, j).start()
        sg_buf[1, j] = go_ref[:, cols].astype(jnp.float32) * q_ref[:, cols].astype(jnp.float32)
        swap(1, j).start()
        return carry

    lax.fori_loop(0, chunks, gate_out, 0)

    def filter_copy(d):
        target = (me + d) % groups
        part = pl.ds(pl.multiple_of((target % 2) * nf, nf), nf)
        return remote(filt_ref.at[part, :], h_buf.at[z, c], f_send.at[d], f_recv.at[d], target)

    for d in range(1, groups):
        filter_copy(d).start()
    h_buf[z, c] = filt_ref[pl.ds(pl.multiple_of(c * nf, nf), nf), :]

    def gate_own(j, carry):
        cols = columns(c, j)
        g_buf[0, j, my_rows, :] = k_ref[:, cols].astype(jnp.float32) * v_ref[:, cols].astype(jnp.float32)
        r_buf[0, j, my_rows, :] = go_ref[:, cols].astype(jnp.float32) * q_ref[:, cols].astype(jnp.float32)
        return carry

    lax.fori_loop(0, chunks, gate_own, 0)

    def g_copy(s, j):
        return remote(g_buf.at[s, j], g_buf.at[s + 1, j], g_send.at[s, j], g_recv.at[s, j], right)

    def r_copy(s, j):
        return remote(r_buf.at[s, j], r_buf.at[s + 1, j], r_send.at[s, j], r_recv.at[s, j], left)

    def first_sends(j, carry):
        swap(0, j).wait_recv()

        @pl.when(z + 1 < chips)
        def _():
            g_copy(0, j).start()

        swap(1, j).wait_recv()

        @pl.when(z >= 1)
        def _():
            r_copy(0, j).start()
        return carry

    lax.fori_loop(0, chunks, first_sends, 0)

    for load in loads[5:]:
        load.wait()
    for d in range(1, groups):
        filter_copy(d).wait_recv()

    lags = chips * nf
    taps = halves(jnp.concatenate(
        [h_buf[:, 0].reshape(lags, rows), h_buf[:, 1].reshape(lags, rows)], axis=1))
    wide = dot(fwd_hi[:, block:], jnp.concatenate(taps, axis=0), NT)
    spec = wide[:, :lags] + wide[:, lags:] + dot(fwd_lo[:, block:], taps[0], NT)
    early = jnp.concatenate([jnp.zeros((2 * block, nf), jnp.float32), spec[:, :lags - nf]], axis=1)
    sign = (1 - 2 * (lax.broadcasted_iota(jnp.int32, (block, lags), 0) % 2)).astype(jnp.float32)
    spec = jnp.concatenate(
        [spec[:block] - sign * early[block:], spec[block:] + sign * early[:block]], axis=0)
    spec = jnp.concatenate(halves(spec), axis=1)

    def widen(m, carry):
        full = dot(spec, spread_ref[m])
        for j in range(chunks):
            h_spec[m, j] = full[:, j * LANES:(j + 1) * LANES]
        return carry

    lax.fori_loop(0, chips, widen, 0)
    c_spec[...] = jnp.zeros_like(c_spec)

    def spectrum(signal):
        return dot3((fwd_hi[:, block:], fwd_lo[:, block:]), halves(signal))

    def conj_times(a, b):
        ar, ai, br, bi = a[:block], a[block:], b[:block], b[block:]
        return jnp.concatenate([ar * br + ai * bi, ar * bi - ai * br], axis=0)

    def times(a, b):
        ar, ai, br, bi = a[:block], a[block:], b[:block], b[block:]
        return jnp.concatenate([ar * br - ai * bi, ar * bi + ai * br], axis=0)

    def add_corr(m, j, g, r):
        prod = jnp.concatenate(halves(conj_times(g, r)), axis=1)
        c_spec[...] += dot(prod, gather_ref[m, j])

    def own_step(j, carry):
        r = spectrum(r_buf[0, j])
        r_spec[j] = r
        gg_acc[j] = conj_times(h_spec[0, j], r)
        g = spectrum(g_buf[0, j])
        conv_acc[j] = times(h_spec[0, j], g)
        add_corr(0, j, g, r)
        return carry

    lax.fori_loop(0, chunks, own_step, 0)

    def y_copy(which, j):
        return remote(y_buf.at[which, j, its_rows, :], x_buf.at[which, j],
                      y_send.at[which, j], y_recv.at[which, j], partner)

    def inverse(spec):
        return dot3((inv_hi[...], inv_lo[...]), halves(spec))

    def part_copy(which, j):
        if which == 0:
            return remote(part_buf.at[0, j], g_buf.at[2, j], g_send.at[1, j], g_recv.at[1, j], right)
        return remote(part_buf.at[1, j], r_buf.at[2, j], r_send.at[1, j], r_recv.at[1, j], left)

    def finish(j):
        for which, near, end in ((0, chips - 2, chips - 1), (1, 1, 0)):
            @pl.when(z == near)
            def _():
                part_buf[which, j] = inverse(part_acc[which, j])
                part_copy(which, j).start()

        for which, acc, out, end in ((0, conv_acc, conv_ref, chips - 1), (1, gg_acc, gg_ref, 0)):
            y_buf[which, j] = inverse(acc[j])

            @pl.when(z == end)
            def _():
                part_copy(which, j).wait_recv()
                y_buf[which, j] += (g_buf if which == 0 else r_buf)[2, j]

            y_copy(which, j).start()
            out[:, columns(c, j)] = y_buf[which, j, my_rows, :]

    last_step = chips - 3
    for s in range(last_step + 1):
        def step(j, carry):
            @pl.when((z + 1 + s < chips) & ((z >= 1) | (s == 0)))
            def _():
                r_copy(s, j).wait_recv()
                if s < last_step:
                    @pl.when(z >= 2)
                    def _():
                        r_copy(s + 1, j).start()
                r = spectrum(r_buf[s + 1, j])
                gg_acc[j] += conj_times(h_spec[s + 1, j], r)
                if s == 0:
                    r_next[j] = r

                @pl.when(z == 1)
                def _():
                    term = conj_times(h_spec[s + 2, j], r)
                    part_acc[1, j] = term if s == 0 else part_acc[1, j] + term

            @pl.when((z - 1 - s >= 0) & ((z <= chips - 2) | (s == 0)))
            def _():
                g_copy(s, j).wait_recv()
                if s < last_step:
                    @pl.when(z <= chips - 3)
                    def _():
                        g_copy(s + 1, j).start()
                g = spectrum(g_buf[s + 1, j])
                conv_acc[j] += times(h_spec[s + 1, j], g)
                add_corr(s + 1, j, g, r_spec[j])

                @pl.when(z == chips - 2)
                def _():
                    term = times(h_spec[s + 2, j], g)
                    part_acc[0, j] = term if s == 0 else part_acc[0, j] + term
                    add_corr(s + 2, j, g, r_next[j])

            if s == last_step:
                finish(j)
            return carry

        lax.fori_loop(0, chunks, step, 0)

    corr = halves(c_spec[...])
    both = jnp.concatenate(corr, axis=1)
    wide = dot(both, fwd_hi[...], TN)
    turned = wide[:lags] + wide[lags:] + dot(corr[0], fwd_lo[...], TN)
    below = jnp.concatenate([turned[nf:, :block], jnp.zeros((nf, block), jnp.float32)], axis=0)
    sums = (turned[:, block:] + below) * (1.0 / block)

    def c_copy(n):
        return remote(c_own.at[n], c_buf.at[z], c_send.at[n], c_recv.at[z], n * 2 + c)

    my_reach = jnp.where(z == chips - 2, chips - 1, jnp.where(z == chips - 1, 1, z))

    def reach(chip):
        return {chips - 2: chips - 1, chips - 1: 1}.get(chip, chip)

    for n in range(chips):
        c_own[n, 0] = sums[n * nf:(n + 1) * nf, :rows]
        c_own[n, 1] = sums[n * nf:(n + 1) * nf, rows:]

        @pl.when((n <= my_reach) & (n != z))
        def _():
            c_copy(n).start()

    for i in range(1, chips):
        @pl.when((z <= reach(i)) & (i != z))
        def _():
            remote(c_own.at[0], c_buf.at[i], c_send.at[0], c_recv.at[i], partner).wait_recv()
            c_own[z] += c_buf[i]

    last = remote(c_own.at[z, 1 - c], f_buf, p_send, p_recv, partner)
    last.start()
    gf_ref[pl.ds(pl.multiple_of(c * nf, nf), nf), :] = c_own[z, c]

    def place(j, carry):
        for which, out in ((0, conv_ref), (1, gg_ref)):
            y_copy(which, j).wait_recv()
            out[:, columns(1 - c, j)] = x_buf[which, j]
        return carry

    lax.fori_loop(0, chunks, place, 0)
    last.wait_recv()
    gf_ref[pl.ds(pl.multiple_of((1 - c) * nf, nf), nf), :] = f_buf[...]

    last.wait_send()
    for n in range(chips):
        @pl.when((n <= my_reach) & (n != z))
        def _():
            c_copy(n).wait_send()
    for d in range(1, groups):
        filter_copy(d).wait_send()

    def drain(j, carry):
        for which in range(2):
            swap(which, j).wait_send()
            y_copy(which, j).wait_send()
        for s in range(last_step + 1):
            @pl.when((z - s >= 0) & (z + 1 < (chips if s == 0 else chips - 1)))
            def _():
                g_copy(s, j).wait_send()

            @pl.when((z + s < chips) & (z >= (1 if s == 0 else 2)))
            def _():
                r_copy(s, j).wait_send()

        for which, near in ((0, chips - 2), (1, 1)):
            @pl.when(z == near)
            def _():
                part_copy(which, j).wait_send()
        return carry

    lax.fori_loop(0, chunks, drain, 0)


def scratch(chips, rows, half, nf):
    chunks, block = half // LANES, 2 * rows
    f32 = jnp.float32
    memory = [
        (chips, chunks, block, LANES),
        (chips, chunks, block, LANES),
        (2, chunks, rows, LANES),
        (chips, 2, nf, rows),
        (chips, chunks, 2 * block, LANES),
        (chunks, 2 * block, LANES),
        (chunks, 2 * block, LANES),
        (chunks, 2 * block, LANES),
        (chunks, 2 * block, LANES),
        (2, chunks, 2 * block, LANES),
        (2, chunks, block, LANES),
        (2 * block, chips * nf),
        (2, chunks, block, LANES),
        (2, chunks, rows, LANES),
        (chips, 2, nf, rows),
        (chips, 2, nf, rows),
        (nf, rows),
    ]
    steps = max(chips - 1, 1)
    sems = [
        (2 * chips,), (2 * chips,), (2, chunks), (2, chunks), (steps, chunks), (steps, chunks),
        (steps, chunks), (steps, chunks), (2, chunks), (2, chunks), (chips,), (chips,),
        (11,),
    ]
    used = sum(4 * math.prod(shape) for shape in memory)
    held = [((rows, 2 * half), jnp.bfloat16)] * 4 + [((2 * nf, rows), f32)]
    held += [((2 * block, 2 * block), jnp.bfloat16)] * 2 + [((block, 2 * block), jnp.bfloat16)] * 2
    held += [((chips, 2 * chips * nf, half), jnp.bfloat16), ((chips, chunks, 2 * LANES, chips * nf), jnp.bfloat16)]
    specs = [pltpu.VMEM(shape, kind) for shape, kind in held]
    specs += [pltpu.VMEM(shape, f32) for shape in memory]
    specs += [pltpu.SemaphoreType.DMA(shape) for shape in sems]
    specs += [pltpu.SemaphoreType.DMA, pltpu.SemaphoreType.DMA]
    return used, specs


def fits(chips, rows, width, filters):
    used, _ = scratch(chips, rows, width // 2, filters // 2)
    aligned = rows % LANES == 0 and chips * filters == 2 * LANES and width % (2 * LANES) == 0 and filters % 16 == 0
    return aligned and chips >= 3 and used <= VMEM_BUDGET // 2


def local_fast(query_gate, key_gate, value_in, filter_raw, grad_out):
    groups = lax.axis_size("context")
    chips = groups // 2
    rows, width = query_gate.shape
    filters = filter_raw.shape[1]
    half, nf, block = width // 2, filters // 2, 2 * rows
    chunks = half // LANES
    scale = 1.0 / math.sqrt(groups * rows)
    forward = tables(block)
    fwd = np_halves(forward)
    inv = np_halves(forward[:, block:].T / block)
    member = np.kron(np.eye(chips * nf), np.ones((1, width // filters)))
    member = member.reshape(chips * nf, chips, half).transpose(1, 0, 2)
    spread = np.tile(member, (1, 2, 1)).astype(jnp.bfloat16)
    gather = member.reshape(chips, chips * nf, chunks, LANES).transpose(0, 2, 3, 1)
    gather = np.tile(gather, (1, 1, 2, 1)).astype(jnp.bfloat16)
    _, scratches = scratch(chips, rows, half, nf)
    vmem = pl.BlockSpec(memory_space=pltpu.VMEM)
    conv, grad_gated, corr = pl.pallas_call(
        functools.partial(kernel, chips),
        out_shape=(
            jax.ShapeDtypeStruct((rows, width), jnp.float32),
            jax.ShapeDtypeStruct((rows, width), jnp.float32),
            jax.ShapeDtypeStruct((filters, rows), jnp.float32),
        ),
        in_specs=[pl.BlockSpec(memory_space=pltpu.HBM)] * 11,
        out_specs=(vmem,) * 3,
        scratch_shapes=scratches,
        compiler_params=pltpu.CompilerParams(
            collective_id=0, has_side_effects=True, vmem_limit_bytes=VMEM_LIMIT),
        cost_estimate=pl.CostEstimate(flops=10**10, bytes_accessed=8 * 2**20, transcendentals=0),
        name="ring_conv",
    )(query_gate, key_gate, value_in, grad_out, (filter_raw * scale).T, *fwd, *inv, spread, gather)
    output = (query_gate.astype(jnp.float32) * conv).astype(jnp.bfloat16)
    grad_query = (grad_out.astype(jnp.float32) * conv).astype(jnp.bfloat16)
    grad_key = (grad_gated * value_in.astype(jnp.float32)).astype(jnp.bfloat16)
    grad_value = (grad_gated * key_gate.astype(jnp.float32)).astype(jnp.bfloat16)
    return output, grad_query, grad_key, grad_value, corr.T * scale


def dispatch(query_gate, key_gate, value_in, filter_raw, grad_out):
    args = (query_gate, key_gate, value_in, filter_raw, grad_out)
    rows, width = query_gate.shape
    if fits(lax.axis_size("context") // 2, rows, width, filter_raw.shape[1]):
        return local_fast(*args)
    return local(*args)


def solution(mesh):
    return jax.shard_map(
        dispatch,
        mesh=mesh,
        in_specs=(
            P("context", "tensor"),
            P("context", "tensor"),
            P("context", "tensor"),
            P("context", "tensor"),
            P("context", "tensor"),
        ),
        out_specs=(
            P("context", "tensor"),
            P("context", "tensor"),
            P("context", "tensor"),
            P("context", "tensor"),
            P("context", "tensor"),
        ),
        check_vma=False,
    )
```

```python
import functools
import math

import jax
import jax.numpy as jnp
import numpy as np
from jax import lax
from jax.experimental import pallas as pl
from jax.experimental.pallas import tpu as pltpu
from jax.sharding import PartitionSpec as P

highest = lax.Precision.HIGHEST


def phase_table(count_rows, count_cols, period):
    row_index = lax.broadcasted_iota(jnp.int32, (count_rows, count_cols), 0)
    col_index = lax.broadcasted_iota(jnp.int32, (count_rows, count_cols), 1)
    return (row_index * col_index % period).astype(jnp.float32) * (2.0 * math.pi / period)


def rotate(real_part, imag_part, cosine, sine):
    return (real_part * cosine - imag_part * sine, real_part * sine + imag_part * cosine)


def local(query_gate, key_gate, value_in, filter_raw, grad_out):
    groups = lax.axis_size("context")
    here = lax.axis_index("context")
    rows = query_gate.shape[0]
    width = query_gate.shape[1]
    filter_count = filter_raw.shape[1]
    group_size = width // filter_count
    points = 2 * groups * rows
    scale = 1.0 / math.sqrt(groups * rows)
    local_phase = phase_table(rows, rows, rows)
    cos_local = jnp.cos(local_phase)
    sin_local = jnp.sin(local_phase)
    row_iota = lax.broadcasted_iota(jnp.int32, (1, rows, 1), 1)
    parity = lax.broadcasted_iota(jnp.int32, (2, 1, 1), 0)

    def twiddle_phase(first):
        frequency = 2 * first + parity
        return (row_iota * frequency % points).astype(jnp.float32) * (2.0 * math.pi / points)

    def transpose_forward(signal):
        pieces = lax.all_to_all(signal[None], "context", split_axis=1, concat_axis=0, tiled=True)
        angles = phase_table(2 * groups, groups, 2 * groups)
        spread_re = jnp.einsum("ap,plc->alc", jnp.cos(angles), pieces, precision=highest)
        spread_im = -jnp.einsum("ap,plc->alc", jnp.sin(angles), pieces, precision=highest)
        return lax.all_to_all(
            jnp.stack([spread_re, spread_im]), "context", split_axis=1, concat_axis=2, tiled=True
        )

    def forward(signal):
        spec = transpose_forward(signal)
        phase = twiddle_phase(here)
        tw_re, tw_im = rotate(spec[0], spec[1], jnp.cos(phase), -jnp.sin(phase))
        out_re = jnp.einsum("br,erc->ebc", cos_local, tw_re, precision=highest) + jnp.einsum(
            "br,erc->ebc", sin_local, tw_im, precision=highest
        )
        out_im = jnp.einsum("br,erc->ebc", cos_local, tw_im, precision=highest) - jnp.einsum(
            "br,erc->ebc", sin_local, tw_re, precision=highest
        )
        return jnp.stack([out_re, out_im])

    def transpose_inverse(spec):
        pieces = lax.all_to_all(spec, "context", split_axis=2, concat_axis=1, tiled=True)
        angles = phase_table(groups, 2 * groups, 2 * groups)
        values = jnp.einsum(
            "pa,alc->plc", jnp.cos(angles), pieces[0], precision=highest
        ) - jnp.einsum("pa,alc->plc", jnp.sin(angles), pieces[1], precision=highest)
        return lax.all_to_all(values, "context", split_axis=0, concat_axis=1, tiled=True)[0]

    def turned(spec, first):
        loc_re = jnp.einsum("rb,ebc->erc", cos_local, spec[0], precision=highest) - jnp.einsum(
            "rb,ebc->erc", sin_local, spec[1], precision=highest
        )
        loc_im = jnp.einsum("rb,ebc->erc", cos_local, spec[1], precision=highest) + jnp.einsum(
            "rb,ebc->erc", sin_local, spec[0], precision=highest
        )
        phase = twiddle_phase(first)
        rot_re, rot_im = rotate(loc_re, loc_im, jnp.cos(phase), jnp.sin(phase))
        return jnp.stack([rot_re, rot_im])

    def inverse(spec):
        signal = transpose_inverse(turned(spec, here))
        return signal * (1.0 / points)

    def widen(part):
        spread = jnp.broadcast_to(part[..., None], part.shape + (group_size,))
        return spread.reshape(part.shape[:-1] + (width,))

    def group_total(part):
        return jnp.sum(part.reshape(part.shape[:-1] + (filter_count, group_size)), axis=-1)

    query_full = query_gate.astype(jnp.float32)
    key_full = key_gate.astype(jnp.float32)
    value_full = value_in.astype(jnp.float32)
    grad_full = grad_out.astype(jnp.float32)
    gated = key_full * value_full
    grad_conv = grad_full * query_full
    filt_part = filter_raw * scale
    spec_gated = forward(gated)
    spec_grad = forward(grad_conv)
    spec_filt = forward(filt_part)
    gated_re, gated_im = (spec_gated[0], spec_gated[1])
    filt_re, filt_im = (widen(spec_filt[0]), widen(spec_filt[1]))
    grad_re, grad_im = (spec_grad[0], spec_grad[1])
    conv_spec = jnp.stack(
        [gated_re * filt_re - gated_im * filt_im, gated_re * filt_im + gated_im * filt_re]
    )
    back_spec = jnp.stack(
        [filt_re * grad_re + filt_im * grad_im, filt_re * grad_im - filt_im * grad_re]
    )
    corr_spec = jnp.stack(
        [
            group_total(gated_re * grad_re + gated_im * grad_im),
            group_total(gated_re * grad_im - gated_im * grad_re),
        ]
    )
    conv = inverse(conv_spec)
    grad_gated = inverse(back_spec)
    corr = inverse(corr_spec)
    output = (query_full * conv).astype(jnp.bfloat16)
    grad_query = (grad_full * conv).astype(jnp.bfloat16)
    grad_key = (grad_gated * value_full).astype(jnp.bfloat16)
    grad_value = (grad_gated * key_full).astype(jnp.bfloat16)
    grad_filter = corr * scale
    return (output, grad_query, grad_key, grad_value, grad_filter)


LANES = 128
VMEM_BUDGET = 40 * 2**20
VMEM_LIMIT = 60 * 2**20


def halves(table):
    high = jnp.asarray(table, jnp.float32).astype(jnp.bfloat16)
    low = (jnp.asarray(table, jnp.float32) - high.astype(jnp.float32)).astype(jnp.bfloat16)
    return high, low


def np_halves(table):
    table = table.astype(np.float32)
    high = table.astype(jnp.bfloat16)
    low = (table - high.astype(np.float32)).astype(jnp.bfloat16)
    return high, low


def tables(block):
    k = np.arange(block, dtype=np.float64)[:, None] + 0.5
    n = np.arange(-block, block, dtype=np.float64)[None, :]
    angle = (np.pi / block) * k * n
    return np.concatenate([np.cos(angle), -np.sin(angle)], axis=0)


NN = (((1,), (0,)), ((), ()))
NT = (((1,), (1,)), ((), ()))
TN = (((0,), (0,)), ((), ()))


def dot(a, b, dims=NN):
    return lax.dot_general(a, b, dims, preferred_element_type=jnp.float32)


def dot3(a, b):
    count = b[0].shape[1]
    wide = dot(a[0], jnp.concatenate(b, axis=1))
    return wide[:, :count] + wide[:, count:] + dot(a[1], b[0])


def kernel(chips, scale, q_hbm, k_hbm, v_hbm, go_hbm, filt_hbm, fwd_hi_hbm, fwd_lo_hbm, inv_hi_hbm, inv_lo_hbm, spread_hbm, gather_hbm,
           conv_ref, gg_ref, gf_ref,
           q_ref, k_ref, v_ref, go_ref, filt_ref, fwd_hi, fwd_lo, inv_hi, inv_lo, spread_ref, gather_ref,
           g_buf, r_buf, sg_buf, h_buf, h_spec, conv_acc, gg_acc, r_spec, r_next, part_acc, part_buf, c_spec, y_buf, x_buf, c_own, c_buf, end_buf,
           f_send, f_recv, e_send, e_recv, g_send, g_recv, r_send, r_recv, y_send, y_recv, c_send, c_recv, load_sem, o_send, o_recv, p_send, p_recv):
    groups = 2 * chips
    rows = q_ref.shape[0]
    half = q_ref.shape[1] // 2
    block = 2 * rows
    chunks = half // LANES
    nf = filt_ref.shape[0] // 2
    me = lax.axis_index("context")
    z, c = me // 2, me % 2
    partner = z * 2 + (1 - c)
    right = (me + 2) % groups
    left = (me + groups - 2) % groups

    def remote(src, dst, send, recv, target):
        return pltpu.make_async_remote_copy(
            src_ref=src, dst_ref=dst, send_sem=send, recv_sem=recv,
            device_id={"context": target}, device_id_type=pl.DeviceIdType.MESH)

    def columns(which, j):
        return pl.ds(pl.multiple_of(which * half + j * LANES, LANES), LANES)

    my_rows = pl.ds(pl.multiple_of(c * rows, rows), rows)
    its_rows = pl.ds(pl.multiple_of((1 - c) * rows, rows), rows)

    loads = [pltpu.make_async_copy(src, dst, load_sem.at[i]) for i, (src, dst) in enumerate((
        (k_hbm, k_ref), (v_hbm, v_ref), (go_hbm, go_ref), (q_hbm, q_ref), (filt_hbm, filt_ref),
        (fwd_hi_hbm, fwd_hi), (fwd_lo_hbm, fwd_lo), (spread_hbm, spread_ref), (gather_hbm, gather_ref), (inv_hi_hbm, inv_hi),
        (inv_lo_hbm, inv_lo)))]
    for load in loads:
        load.start()

    barrier = pltpu.get_barrier_semaphore()
    for d in range(1, groups):
        pl.semaphore_signal(barrier, inc=1, device_id={"context": (me + d) % groups},
                            device_id_type=pl.DeviceIdType.MESH)
    def swap(which, j):
        buf = g_buf if which == 0 else r_buf
        return remote(sg_buf.at[which, j], buf.at[0, j, my_rows, :],
                      e_send.at[which, j], e_recv.at[which, j], partner)

    for load in loads[:5]:
        load.wait()

    def gate(j, carry):
        cols = columns(1 - c, j)
        sg_buf[0, j] = k_ref[:, cols].astype(jnp.float32) * v_ref[:, cols].astype(jnp.float32)
        sg_buf[1, j] = go_ref[:, cols].astype(jnp.float32) * q_ref[:, cols].astype(jnp.float32)
        cols = columns(c, j)
        g_buf[0, j, my_rows, :] = k_ref[:, cols].astype(jnp.float32) * v_ref[:, cols].astype(jnp.float32)
        r_buf[0, j, my_rows, :] = go_ref[:, cols].astype(jnp.float32) * q_ref[:, cols].astype(jnp.float32)
        return carry

    lax.fori_loop(0, chunks, gate, 0)
    pl.semaphore_wait(barrier, groups - 1)

    def filter_copy(d):
        target = (me + d) % groups
        part = pl.ds(pl.multiple_of((target % 2) * nf, nf), nf)
        return remote(filt_ref.at[part, :], h_buf.at[z, c], f_send.at[d], f_recv.at[d], target)

    for d in range(1, groups):
        filter_copy(d).start()
    h_buf[z, c] = filt_ref[pl.ds(pl.multiple_of(c * nf, nf), nf), :]

    def own_copy(which, other, j):
        buf = g_buf if which == 0 else r_buf
        near = partner if other else me
        target = (near + 2) % groups if which == 0 else (near + groups - 2) % groups
        return remote(sg_buf.at[which, j] if other else buf.at[0, j, my_rows, :], buf.at[1, j, my_rows, :],
                      o_send.at[which, other, j], o_recv.at[which, c, j], target)

    def own_wait(which, j):
        buf = g_buf if which == 0 else r_buf
        for core in range(2):
            remote(sg_buf.at[which, j], buf.at[1, j, core * rows:(core + 1) * rows, :],
                   o_send.at[which, 0, j], o_recv.at[which, core, j], partner).wait_recv()

    def g_copy(s, j):
        return remote(g_buf.at[s, j], g_buf.at[s + 1, j], g_send.at[s, j], g_recv.at[s, j], right)

    def r_copy(s, j):
        return remote(r_buf.at[s, j], r_buf.at[s + 1, j], r_send.at[s, j], r_recv.at[s, j], left)

    def first_sends(j, carry):
        swap(0, j).start()
        swap(1, j).start()

        @pl.when(z + 1 < chips)
        def _():
            own_copy(0, 0, j).start()
            own_copy(0, 1, j).start()

        @pl.when(z >= 1)
        def _():
            own_copy(1, 0, j).start()
            own_copy(1, 1, j).start()
        return carry

    lax.fori_loop(0, chunks, first_sends, 0)

    for load in loads[5:]:
        load.wait()
    for d in range(1, groups):
        filter_copy(d).wait_recv()

    lags = chips * nf
    taps = halves(jnp.concatenate(
        [h_buf[:, 0].reshape(lags, rows), h_buf[:, 1].reshape(lags, rows)], axis=1) * scale)
    wide = dot(fwd_hi[:, block:], jnp.concatenate(taps, axis=0), NT)
    spec = wide[:, :lags] + wide[:, lags:] + dot(fwd_lo[:, block:], taps[0], NT)
    early = jnp.concatenate([jnp.zeros((2 * block, nf), jnp.float32), spec[:, :lags - nf]], axis=1)
    sign = (1 - 2 * (lax.broadcasted_iota(jnp.int32, (block, lags), 0) % 2)).astype(jnp.float32)
    spec = jnp.concatenate(
        [spec[:block] - sign * early[block:], spec[block:] + sign * early[:block]], axis=0)
    spec = jnp.concatenate(halves(spec), axis=1)

    def widen(m, carry):
        full = dot(spec, spread_ref[m])
        for j in range(chunks):
            h_spec[m, j] = full[:, j * LANES:(j + 1) * LANES]
        return carry

    lax.fori_loop(0, chips, widen, 0)
    c_spec[...] = jnp.zeros_like(c_spec)

    def spectrum(signal):
        return dot3((fwd_hi[:, block:], fwd_lo[:, block:]), halves(signal))

    def conj_times(a, b):
        ar, ai, br, bi = a[:block], a[block:], b[:block], b[block:]
        return jnp.concatenate([ar * br + ai * bi, ar * bi - ai * br], axis=0)

    def times(a, b):
        ar, ai, br, bi = a[:block], a[block:], b[:block], b[block:]
        return jnp.concatenate([ar * br - ai * bi, ar * bi + ai * br], axis=0)

    def add_corr(m, j, g, r):
        prod = jnp.concatenate(halves(conj_times(g, r)), axis=1)
        c_spec[...] += dot(prod, gather_ref[m, j])

    def own_step(j, carry):
        swap(0, j).wait_recv()
        swap(1, j).wait_recv()
        r = spectrum(r_buf[0, j])
        r_spec[j] = r
        gg_acc[j] = conj_times(h_spec[0, j], r)
        g = spectrum(g_buf[0, j])
        conv_acc[j] = times(h_spec[0, j], g)
        add_corr(0, j, g, r)
        return carry

    lax.fori_loop(0, chunks, own_step, 0)

    def y_copy(which, j):
        return remote(y_buf.at[which, j, its_rows, :], x_buf.at[which, j],
                      y_send.at[which, j], y_recv.at[which, j], partner)

    def inverse(spec):
        return dot3((inv_hi[...], inv_lo[...]), halves(spec))

    def part_copy(which, core, j):
        chip = (z + 1 if which == 0 else z + chips - 1) % chips
        return remote(part_buf.at[which, j, core * rows:(core + 1) * rows, :], end_buf.at[which, c, j],
                      p_send.at[which, core, j], p_recv.at[which, c, j], chip * 2 + core)

    def finish(j):
        for which, near in ((0, chips - 2), (1, 1)):
            @pl.when(z == near)
            def _():
                part_buf[which, j] = inverse(part_acc[which, j])
                part_copy(which, 0, j).start()
                part_copy(which, 1, j).start()

        for which, acc, out in ((0, conv_acc, conv_ref), (1, gg_acc, gg_ref)):
            y_buf[which, j] = inverse(acc[j])
            y_copy(which, j).start()
            out[:, columns(c, j)] = y_buf[which, j, my_rows, :]

    last_step = chips - 3
    for s in range(last_step + 1):
        def step(j, carry):
            @pl.when((z + 1 + s < chips) & ((z >= 1) | (s == 0)))
            def _():
                own_wait(1, j) if s == 0 else r_copy(s, j).wait_recv()
                if s < last_step:
                    @pl.when(z >= 2)
                    def _():
                        r_copy(s + 1, j).start()
                r = spectrum(r_buf[s + 1, j])
                gg_acc[j] += conj_times(h_spec[s + 1, j], r)
                if s == 0:
                    r_next[j] = r

                @pl.when(z == 1)
                def _():
                    term = conj_times(h_spec[s + 2, j], r)
                    part_acc[1, j] = term if s == 0 else part_acc[1, j] + term

            @pl.when((z - 1 - s >= 0) & ((z <= chips - 2) | (s == 0)))
            def _():
                own_wait(0, j) if s == 0 else g_copy(s, j).wait_recv()
                if s < last_step:
                    @pl.when(z <= chips - 3)
                    def _():
                        g_copy(s + 1, j).start()
                g = spectrum(g_buf[s + 1, j])
                conv_acc[j] += times(h_spec[s + 1, j], g)
                add_corr(s + 1, j, g, r_spec[j])

                @pl.when(z == chips - 2)
                def _():
                    term = times(h_spec[s + 2, j], g)
                    part_acc[0, j] = term if s == 0 else part_acc[0, j] + term
                    add_corr(s + 2, j, g, r_next[j])

            if s == last_step:
                finish(j)
            return carry

        lax.fori_loop(0, chunks, step, 0)

    corr = halves(c_spec[...])
    both = jnp.concatenate(corr, axis=1)
    wide = dot(both, fwd_hi[...], TN)
    turned = wide[:lags] + wide[lags:] + dot(corr[0], fwd_lo[...], TN)
    below = jnp.concatenate([turned[nf:, :block], jnp.zeros((nf, block), jnp.float32)], axis=0)
    sums = (turned[:, block:] + below) * (1.0 / block)

    def c_copy(n, core):
        return remote(c_own.at[n, core], c_buf.at[z, c], c_send.at[n, core], c_recv.at[z, c], n * 2 + core)

    my_reach = jnp.where(z == chips - 2, chips - 1, jnp.where(z == chips - 1, 1, z))

    def reach(chip):
        return {chips - 2: chips - 1, chips - 1: 1}.get(chip, chip)

    for n in range(chips):
        c_own[n, 0] = sums[n * nf:(n + 1) * nf, :rows]
        c_own[n, 1] = sums[n * nf:(n + 1) * nf, rows:]

        @pl.when((n <= my_reach) & (n != z))
        def _():
            c_copy(n, 0).start()
            c_copy(n, 1).start()

    c_copy(z, 1 - c).start()

    def place(j, carry):
        for which, out, end in ((0, conv_ref, chips - 1), (1, gg_ref, 0)):
            y_copy(which, j).wait_recv()
            out[:, columns(1 - c, j)] = x_buf[which, j]

            @pl.when(z == end)
            def _():
                for core in range(2):
                    remote(part_buf.at[which, j, :rows, :], end_buf.at[which, core, j],
                           p_send.at[which, 0, j], p_recv.at[which, core, j], partner).wait_recv()
                    out[:, columns(core, j)] += end_buf[which, core, j]
        return carry

    lax.fori_loop(0, chunks, place, 0)

    def c_wait(chip, core):
        remote(c_own.at[0, 0], c_buf.at[chip, core], c_send.at[0, 0], c_recv.at[chip, core], partner).wait_recv()

    c_wait(z, 1 - c)
    gf_ref[pl.ds(pl.multiple_of(c * nf, nf), nf), :] = c_own[z, c]
    gf_ref[pl.ds(pl.multiple_of((1 - c) * nf, nf), nf), :] = c_buf[z, 1 - c]
    for i in range(1, chips):
        @pl.when((z <= reach(i)) & (i != z))
        def _():
            for core in range(2):
                c_wait(i, core)
                gf_ref[core * nf:(core + 1) * nf, :] += c_buf[i, core]

    c_copy(z, 1 - c).wait_send()
    for n in range(chips):
        @pl.when((n <= my_reach) & (n != z))
        def _():
            c_copy(n, 0).wait_send()
            c_copy(n, 1).wait_send()
    for d in range(1, groups):
        filter_copy(d).wait_send()

    def drain(j, carry):
        for which in range(2):
            swap(which, j).wait_send()
            y_copy(which, j).wait_send()
        for which, sends in ((0, z + 1 < chips), (1, z >= 1)):
            @pl.when(sends)
            def _():
                own_copy(which, 0, j).wait_send()
                own_copy(which, 1, j).wait_send()

        for s in range(1, last_step + 1):
            @pl.when((z - s >= 0) & (z + 1 < chips - 1))
            def _():
                g_copy(s, j).wait_send()

            @pl.when((z + s < chips) & (z >= 2))
            def _():
                r_copy(s, j).wait_send()

        for which, near in ((0, chips - 2), (1, 1)):
            @pl.when(z == near)
            def _():
                part_copy(which, 0, j).wait_send()
                part_copy(which, 1, j).wait_send()
        return carry

    lax.fori_loop(0, chunks, drain, 0)


def scratch(chips, rows, half, nf):
    chunks, block = half // LANES, 2 * rows
    f32 = jnp.float32
    memory = [
        (chips, chunks, block, LANES),
        (chips, chunks, block, LANES),
        (2, chunks, rows, LANES),
        (chips, 2, nf, rows),
        (chips, chunks, 2 * block, LANES),
        (chunks, 2 * block, LANES),
        (chunks, 2 * block, LANES),
        (chunks, 2 * block, LANES),
        (chunks, 2 * block, LANES),
        (2, chunks, 2 * block, LANES),
        (2, chunks, block, LANES),
        (2 * block, chips * nf),
        (2, chunks, block, LANES),
        (2, chunks, rows, LANES),
        (chips, 2, nf, rows),
        (chips, 2, nf, rows),
        (2, 2, chunks, rows, LANES),
    ]
    steps = max(chips - 1, 1)
    sems = [
        (2 * chips,), (2 * chips,), (2, chunks), (2, chunks), (steps, chunks), (steps, chunks),
        (steps, chunks), (steps, chunks), (2, chunks), (2, chunks), (chips, 2), (chips, 2),
        (11,), (2, 2, chunks), (2, 2, chunks), (2, 2, chunks), (2, 2, chunks),
    ]
    used = sum(4 * math.prod(shape) for shape in memory)
    held = [((rows, 2 * half), jnp.bfloat16)] * 4 + [((2 * nf, rows), f32)]
    held += [((2 * block, 2 * block), jnp.bfloat16)] * 2 + [((block, 2 * block), jnp.bfloat16)] * 2
    held += [((chips, 2 * chips * nf, half), jnp.bfloat16), ((chips, chunks, 2 * LANES, chips * nf), jnp.bfloat16)]
    specs = [pltpu.VMEM(shape, kind) for shape, kind in held]
    specs += [pltpu.VMEM(shape, f32) for shape in memory]
    specs += [pltpu.SemaphoreType.DMA(shape) for shape in sems]
    return used, specs


def fits(chips, rows, width, filters):
    used, _ = scratch(chips, rows, width // 2, filters // 2)
    aligned = rows % LANES == 0 and chips * filters == 2 * LANES and width % (2 * LANES) == 0 and filters % 16 == 0
    return aligned and chips >= 3 and used <= VMEM_BUDGET // 2


def local_fast(query_gate, key_gate, value_in, filter_raw, grad_out):
    groups = lax.axis_size("context")
    chips = groups // 2
    rows, width = query_gate.shape
    filters = filter_raw.shape[1]
    half, nf, block = width // 2, filters // 2, 2 * rows
    chunks = half // LANES
    scale = 1.0 / math.sqrt(groups * rows)
    forward = tables(block)
    fwd = np_halves(forward)
    inv = np_halves(forward[:, block:].T / block)
    member = np.kron(np.eye(chips * nf), np.ones((1, width // filters)))
    member = member.reshape(chips * nf, chips, half).transpose(1, 0, 2)
    spread = np.tile(member, (1, 2, 1)).astype(jnp.bfloat16)
    gather = member.reshape(chips, chips * nf, chunks, LANES).transpose(0, 2, 3, 1)
    gather = np.tile(gather, (1, 1, 2, 1)).astype(jnp.bfloat16)
    _, scratches = scratch(chips, rows, half, nf)
    vmem = pl.BlockSpec(memory_space=pltpu.VMEM)
    conv, grad_gated, corr = pl.pallas_call(
        functools.partial(kernel, chips, scale),
        out_shape=(
            jax.ShapeDtypeStruct((rows, width), jnp.float32),
            jax.ShapeDtypeStruct((rows, width), jnp.float32),
            jax.ShapeDtypeStruct((filters, rows), jnp.float32),
        ),
        in_specs=[pl.BlockSpec(memory_space=pltpu.HBM)] * 11,
        out_specs=(vmem,) * 3,
        scratch_shapes=scratches,
        compiler_params=pltpu.CompilerParams(
            collective_id=0, has_side_effects=True, vmem_limit_bytes=VMEM_LIMIT),
        cost_estimate=pl.CostEstimate(flops=10**10, bytes_accessed=8 * 2**20, transcendentals=0),
        name="ring_conv",
    )(query_gate, key_gate, value_in, grad_out, filter_raw.T, *fwd, *inv, spread, gather)
    output = (query_gate.astype(jnp.float32) * conv).astype(jnp.bfloat16)
    grad_query = (grad_out.astype(jnp.float32) * conv).astype(jnp.bfloat16)
    grad_key = (grad_gated * value_in.astype(jnp.float32)).astype(jnp.bfloat16)
    grad_value = (grad_gated * key_gate.astype(jnp.float32)).astype(jnp.bfloat16)
    return output, grad_query, grad_key, grad_value, corr.T * scale


def dispatch(query_gate, key_gate, value_in, filter_raw, grad_out):
    args = (query_gate, key_gate, value_in, filter_raw, grad_out)
    rows, width = query_gate.shape
    if fits(lax.axis_size("context") // 2, rows, width, filter_raw.shape[1]):
        return local_fast(*args)
    return local(*args)


def solution(mesh):
    return jax.shard_map(
        dispatch,
        mesh=mesh,
        in_specs=(
            P("context", "tensor"),
            P("context", "tensor"),
            P("context", "tensor"),
            P("context", "tensor"),
            P("context", "tensor"),
        ),
        out_specs=(
            P("context", "tensor"),
            P("context", "tensor"),
            P("context", "tensor"),
            P("context", "tensor"),
            P("context", "tensor"),
        ),
        check_vma=False,
    )
```

```python
import functools
import math

import jax
import jax.numpy as jnp
import numpy as np
from jax import lax
from jax.experimental import pallas as pl
from jax.experimental.pallas import tpu as pltpu
from jax.sharding import PartitionSpec as P

highest = lax.Precision.HIGHEST


def phase_table(count_rows, count_cols, period):
    row_index = lax.broadcasted_iota(jnp.int32, (count_rows, count_cols), 0)
    col_index = lax.broadcasted_iota(jnp.int32, (count_rows, count_cols), 1)
    return (row_index * col_index % period).astype(jnp.float32) * (2.0 * math.pi / period)


def rotate(real_part, imag_part, cosine, sine):
    return (real_part * cosine - imag_part * sine, real_part * sine + imag_part * cosine)


def local(query_gate, key_gate, value_in, filter_raw, grad_out):
    groups = lax.axis_size("context")
    here = lax.axis_index("context")
    rows = query_gate.shape[0]
    width = query_gate.shape[1]
    filter_count = filter_raw.shape[1]
    group_size = width // filter_count
    points = 2 * groups * rows
    scale = 1.0 / math.sqrt(groups * rows)
    local_phase = phase_table(rows, rows, rows)
    cos_local = jnp.cos(local_phase)
    sin_local = jnp.sin(local_phase)
    row_iota = lax.broadcasted_iota(jnp.int32, (1, rows, 1), 1)
    parity = lax.broadcasted_iota(jnp.int32, (2, 1, 1), 0)

    def twiddle_phase(first):
        frequency = 2 * first + parity
        return (row_iota * frequency % points).astype(jnp.float32) * (2.0 * math.pi / points)

    def transpose_forward(signal):
        pieces = lax.all_to_all(signal[None], "context", split_axis=1, concat_axis=0, tiled=True)
        angles = phase_table(2 * groups, groups, 2 * groups)
        spread_re = jnp.einsum("ap,plc->alc", jnp.cos(angles), pieces, precision=highest)
        spread_im = -jnp.einsum("ap,plc->alc", jnp.sin(angles), pieces, precision=highest)
        return lax.all_to_all(
            jnp.stack([spread_re, spread_im]), "context", split_axis=1, concat_axis=2, tiled=True
        )

    def forward(signal):
        spec = transpose_forward(signal)
        phase = twiddle_phase(here)
        tw_re, tw_im = rotate(spec[0], spec[1], jnp.cos(phase), -jnp.sin(phase))
        out_re = jnp.einsum("br,erc->ebc", cos_local, tw_re, precision=highest) + jnp.einsum(
            "br,erc->ebc", sin_local, tw_im, precision=highest
        )
        out_im = jnp.einsum("br,erc->ebc", cos_local, tw_im, precision=highest) - jnp.einsum(
            "br,erc->ebc", sin_local, tw_re, precision=highest
        )
        return jnp.stack([out_re, out_im])

    def transpose_inverse(spec):
        pieces = lax.all_to_all(spec, "context", split_axis=2, concat_axis=1, tiled=True)
        angles = phase_table(groups, 2 * groups, 2 * groups)
        values = jnp.einsum(
            "pa,alc->plc", jnp.cos(angles), pieces[0], precision=highest
        ) - jnp.einsum("pa,alc->plc", jnp.sin(angles), pieces[1], precision=highest)
        return lax.all_to_all(values, "context", split_axis=0, concat_axis=1, tiled=True)[0]

    def turned(spec, first):
        loc_re = jnp.einsum("rb,ebc->erc", cos_local, spec[0], precision=highest) - jnp.einsum(
            "rb,ebc->erc", sin_local, spec[1], precision=highest
        )
        loc_im = jnp.einsum("rb,ebc->erc", cos_local, spec[1], precision=highest) + jnp.einsum(
            "rb,ebc->erc", sin_local, spec[0], precision=highest
        )
        phase = twiddle_phase(first)
        rot_re, rot_im = rotate(loc_re, loc_im, jnp.cos(phase), jnp.sin(phase))
        return jnp.stack([rot_re, rot_im])

    def inverse(spec):
        signal = transpose_inverse(turned(spec, here))
        return signal * (1.0 / points)

    def widen(part):
        spread = jnp.broadcast_to(part[..., None], part.shape + (group_size,))
        return spread.reshape(part.shape[:-1] + (width,))

    def group_total(part):
        return jnp.sum(part.reshape(part.shape[:-1] + (filter_count, group_size)), axis=-1)

    query_full = query_gate.astype(jnp.float32)
    key_full = key_gate.astype(jnp.float32)
    value_full = value_in.astype(jnp.float32)
    grad_full = grad_out.astype(jnp.float32)
    gated = key_full * value_full
    grad_conv = grad_full * query_full
    filt_part = filter_raw * scale
    spec_gated = forward(gated)
    spec_grad = forward(grad_conv)
    spec_filt = forward(filt_part)
    gated_re, gated_im = (spec_gated[0], spec_gated[1])
    filt_re, filt_im = (widen(spec_filt[0]), widen(spec_filt[1]))
    grad_re, grad_im = (spec_grad[0], spec_grad[1])
    conv_spec = jnp.stack(
        [gated_re * filt_re - gated_im * filt_im, gated_re * filt_im + gated_im * filt_re]
    )
    back_spec = jnp.stack(
        [filt_re * grad_re + filt_im * grad_im, filt_re * grad_im - filt_im * grad_re]
    )
    corr_spec = jnp.stack(
        [
            group_total(gated_re * grad_re + gated_im * grad_im),
            group_total(gated_re * grad_im - gated_im * grad_re),
        ]
    )
    conv = inverse(conv_spec)
    grad_gated = inverse(back_spec)
    corr = inverse(corr_spec)
    output = (query_full * conv).astype(jnp.bfloat16)
    grad_query = (grad_full * conv).astype(jnp.bfloat16)
    grad_key = (grad_gated * value_full).astype(jnp.bfloat16)
    grad_value = (grad_gated * key_full).astype(jnp.bfloat16)
    grad_filter = corr * scale
    return (output, grad_query, grad_key, grad_value, grad_filter)


LANES = 128
VMEM_BUDGET = 40 * 2**20
VMEM_LIMIT = 60 * 2**20


def halves(table):
    high = jnp.asarray(table, jnp.float32).astype(jnp.bfloat16)
    low = (jnp.asarray(table, jnp.float32) - high.astype(jnp.float32)).astype(jnp.bfloat16)
    return high, low


def np_halves(table):
    table = table.astype(np.float32)
    high = table.astype(jnp.bfloat16)
    low = (table - high.astype(np.float32)).astype(jnp.bfloat16)
    return high, low


def tables(block):
    k = np.arange(block, dtype=np.float64)[:, None] + 0.5
    n = np.arange(-block, block, dtype=np.float64)[None, :]
    angle = (np.pi / block) * k * n
    return np.concatenate([np.cos(angle), -np.sin(angle)], axis=0)


NN = (((1,), (0,)), ((), ()))
NT = (((1,), (1,)), ((), ()))
TN = (((0,), (0,)), ((), ()))


def dot(a, b, dims=NN):
    return lax.dot_general(a, b, dims, preferred_element_type=jnp.float32)


def dot3(a, b):
    count = b[0].shape[1]
    wide = dot(a[0], jnp.concatenate(b, axis=1))
    return wide[:, :count] + wide[:, count:] + dot(a[1], b[0])


def kernel(chips, scale, q_hbm, k_hbm, v_hbm, go_hbm, filt_hbm, fwd_hi_hbm, fwd_lo_hbm, inv_hi_hbm, inv_lo_hbm, spread_hbm, gather_hbm,
           conv_ref, gg_ref, gf_ref,
           q_ref, k_ref, v_ref, go_ref, filt_ref, fwd_hi, fwd_lo, inv_hi, inv_lo, spread_ref, gather_ref,
           g_buf, r_buf, sg_buf, h_buf, h_spec, conv_acc, gg_acc, r_spec, r_next, part_acc, part_buf, c_spec, y_buf, x_buf, c_own, c_buf, end_buf,
           f_send, f_recv, e_send, e_recv, g_send, g_recv, r_send, r_recv, y_send, y_recv, c_send, c_recv, load_sem, o_send, o_recv, p_send, p_recv):
    groups = 2 * chips
    rows = q_ref.shape[0]
    half = q_ref.shape[1] // 2
    block = 2 * rows
    chunks = half // LANES
    nf = filt_ref.shape[0] // 2
    me = lax.axis_index("context")
    z, c = me // 2, me % 2
    partner = z * 2 + (1 - c)
    right = (me + 2) % groups
    left = (me + groups - 2) % groups

    def remote(src, dst, send, recv, target):
        return pltpu.make_async_remote_copy(
            src_ref=src, dst_ref=dst, send_sem=send, recv_sem=recv,
            device_id={"context": target}, device_id_type=pl.DeviceIdType.MESH)

    def columns(which, j):
        return pl.ds(pl.multiple_of(which * half + j * LANES, LANES), LANES)

    my_rows = pl.ds(pl.multiple_of(c * rows, rows), rows)
    its_rows = pl.ds(pl.multiple_of((1 - c) * rows, rows), rows)

    loads = [pltpu.make_async_copy(src, dst, load_sem.at[i]) for i, (src, dst) in enumerate((
        (k_hbm, k_ref), (v_hbm, v_ref), (go_hbm, go_ref), (q_hbm, q_ref), (filt_hbm, filt_ref),
        (fwd_hi_hbm, fwd_hi), (fwd_lo_hbm, fwd_lo), (spread_hbm, spread_ref), (gather_hbm, gather_ref), (inv_hi_hbm, inv_hi),
        (inv_lo_hbm, inv_lo)))]
    for load in loads:
        load.start()

    barrier = pltpu.get_barrier_semaphore()
    for d in range(1, groups):
        pl.semaphore_signal(barrier, inc=1, device_id={"context": (me + d) % groups},
                            device_id_type=pl.DeviceIdType.MESH)
    def swap(which, j):
        buf = g_buf if which == 0 else r_buf
        return remote(sg_buf.at[which, j], buf.at[0, j, my_rows, :],
                      e_send.at[which, j], e_recv.at[which, j], partner)

    for load in loads[:5]:
        load.wait()

    def gate(j, carry):
        cols = columns(1 - c, j)
        sg_buf[0, j] = k_ref[:, cols].astype(jnp.float32) * v_ref[:, cols].astype(jnp.float32)
        sg_buf[1, j] = go_ref[:, cols].astype(jnp.float32) * q_ref[:, cols].astype(jnp.float32)
        cols = columns(c, j)
        g_buf[0, j, my_rows, :] = k_ref[:, cols].astype(jnp.float32) * v_ref[:, cols].astype(jnp.float32)
        r_buf[0, j, my_rows, :] = go_ref[:, cols].astype(jnp.float32) * q_ref[:, cols].astype(jnp.float32)
        return carry

    lax.fori_loop(0, chunks, gate, 0)
    pl.semaphore_wait(barrier, groups - 1)

    def filter_copy(d):
        target = (me + d) % groups
        part = pl.ds(pl.multiple_of((target % 2) * nf, nf), nf)
        return remote(filt_ref.at[part, :], h_buf.at[z, c], f_send.at[d], f_recv.at[d], target)

    def wanted(source, target):
        return (target <= chips - 2) & ((target >= 1) | (source <= 1))

    def sends_filter(d):
        return wanted(z, ((me + d) % groups) // 2)

    def gets_filter(d):
        return wanted(((me + groups - d) % groups) // 2, z)

    def filter_pass():
        return remote(h_buf.at[0:2], h_buf.at[0:2], f_send.at[0], f_recv.at[0], right)

    for d in range(1, groups):
        @pl.when(sends_filter(d))
        def _():
            filter_copy(d).start()

    @pl.when((z == 0) | (z == chips - 1))
    def _():
        h_buf[2:] = jnp.zeros((chips - 2, 2, nf, rows), jnp.float32)

    h_buf[z, c] = filt_ref[pl.ds(pl.multiple_of(c * nf, nf), nf), :]

    def own_copy(which, other, j):
        buf = g_buf if which == 0 else r_buf
        near = partner if other else me
        target = (near + 2) % groups if which == 0 else (near + groups - 2) % groups
        return remote(sg_buf.at[which, j] if other else buf.at[0, j, my_rows, :], buf.at[1, j, my_rows, :],
                      o_send.at[which, other, j], o_recv.at[which, c, j], target)

    def own_wait(which, j):
        buf = g_buf if which == 0 else r_buf
        for core in range(2):
            remote(sg_buf.at[which, j], buf.at[1, j, core * rows:(core + 1) * rows, :],
                   o_send.at[which, 0, j], o_recv.at[which, core, j], partner).wait_recv()

    def g_copy(s, j):
        return remote(g_buf.at[s, j], g_buf.at[s + 1, j], g_send.at[s, j], g_recv.at[s, j], right)

    def r_copy(s, j):
        return remote(r_buf.at[s, j], r_buf.at[s + 1, j], r_send.at[s, j], r_recv.at[s, j], left)

    def first_sends(j, carry):
        swap(0, j).start()
        swap(1, j).start()

        @pl.when(z + 1 < chips)
        def _():
            own_copy(0, 0, j).start()
            own_copy(0, 1, j).start()

        @pl.when(z >= 1)
        def _():
            own_copy(1, 0, j).start()
            own_copy(1, 1, j).start()
        return carry

    lax.fori_loop(0, chunks, first_sends, 0)

    for load in loads[5:]:
        load.wait()
    for d in range(1, groups):
        @pl.when(gets_filter(d))
        def _():
            filter_copy(d).wait_recv()

    @pl.when(z == chips - 2)
    def _():
        filter_pass().start()

    @pl.when(z == chips - 1)
    def _():
        filter_pass().wait_recv()

    lags = chips * nf
    taps = halves(jnp.concatenate(
        [h_buf[:, 0].reshape(lags, rows), h_buf[:, 1].reshape(lags, rows)], axis=1) * scale)
    wide = dot(fwd_hi[:, block:], jnp.concatenate(taps, axis=0), NT)
    spec = wide[:, :lags] + wide[:, lags:] + dot(fwd_lo[:, block:], taps[0], NT)
    early = jnp.concatenate([jnp.zeros((2 * block, nf), jnp.float32), spec[:, :lags - nf]], axis=1)
    sign = (1 - 2 * (lax.broadcasted_iota(jnp.int32, (block, lags), 0) % 2)).astype(jnp.float32)
    spec = jnp.concatenate(
        [spec[:block] - sign * early[block:], spec[block:] + sign * early[:block]], axis=0)
    spec = jnp.concatenate(halves(spec), axis=1)

    def widen(m, carry):
        full = dot(spec, spread_ref[m])
        for j in range(chunks):
            h_spec[m, j] = full[:, j * LANES:(j + 1) * LANES]
        return carry

    lax.fori_loop(0, chips, widen, 0)
    c_spec[...] = jnp.zeros_like(c_spec)

    def spectrum(signal):
        return dot3((fwd_hi[:, block:], fwd_lo[:, block:]), halves(signal))

    def conj_times(a, b):
        ar, ai, br, bi = a[:block], a[block:], b[:block], b[block:]
        return jnp.concatenate([ar * br + ai * bi, ar * bi - ai * br], axis=0)

    def times(a, b):
        ar, ai, br, bi = a[:block], a[block:], b[:block], b[block:]
        return jnp.concatenate([ar * br - ai * bi, ar * bi + ai * br], axis=0)

    def add_corr(m, j, g, r):
        prod = jnp.concatenate(halves(conj_times(g, r)), axis=1)
        c_spec[...] += dot(prod, gather_ref[m, j])

    def own_step(j, carry):
        swap(0, j).wait_recv()
        swap(1, j).wait_recv()
        r = spectrum(r_buf[0, j])
        r_spec[j] = r
        gg_acc[j] = conj_times(h_spec[0, j], r)
        g = spectrum(g_buf[0, j])
        conv_acc[j] = times(h_spec[0, j], g)
        add_corr(0, j, g, r)
        return carry

    lax.fori_loop(0, chunks, own_step, 0)

    def y_copy(which, j):
        return remote(y_buf.at[which, j, its_rows, :], x_buf.at[which, j],
                      y_send.at[which, j], y_recv.at[which, j], partner)

    def inverse(spec):
        return dot3((inv_hi[...], inv_lo[...]), halves(spec))

    def part_copy(which, core, j):
        chip = (z + 1 if which == 0 else z + chips - 1) % chips
        return remote(part_buf.at[which, j, core * rows:(core + 1) * rows, :], end_buf.at[which, c, j],
                      p_send.at[which, core, j], p_recv.at[which, c, j], chip * 2 + core)

    def finish(j):
        for which, near in ((0, chips - 2), (1, 1)):
            @pl.when(z == near)
            def _():
                part_buf[which, j] = inverse(part_acc[which, j])
                part_copy(which, 0, j).start()
                part_copy(which, 1, j).start()

        for which, acc, out in ((0, conv_acc, conv_ref), (1, gg_acc, gg_ref)):
            y_buf[which, j] = inverse(acc[j])
            y_copy(which, j).start()
            out[:, columns(c, j)] = y_buf[which, j, my_rows, :]

    last_step = chips - 3
    for s in range(last_step + 1):
        def step(j, carry):
            r_here = (z + 1 + s < chips) & ((z >= 1) | (s == 0))
            g_here = (z - 1 - s >= 0) & ((z <= chips - 2) | (s == 0))

            @pl.when(r_here)
            def _():
                own_wait(1, j) if s == 0 else r_copy(s, j).wait_recv()
                if s < last_step:
                    @pl.when(z >= 2)
                    def _():
                        r_copy(s + 1, j).start()

            @pl.when(g_here)
            def _():
                own_wait(0, j) if s == 0 else g_copy(s, j).wait_recv()
                if s < last_step:
                    @pl.when(z <= chips - 3)
                    def _():
                        g_copy(s + 1, j).start()

            @pl.when(r_here)
            def _():
                r = spectrum(r_buf[s + 1, j])
                gg_acc[j] += conj_times(h_spec[s + 1, j], r)
                if s == 0:
                    r_next[j] = r

                @pl.when(z == 1)
                def _():
                    term = conj_times(h_spec[s + 2, j], r)
                    part_acc[1, j] = term if s == 0 else part_acc[1, j] + term

            @pl.when(g_here)
            def _():
                g = spectrum(g_buf[s + 1, j])
                conv_acc[j] += times(h_spec[s + 1, j], g)
                add_corr(s + 1, j, g, r_spec[j])

                @pl.when(z == chips - 2)
                def _():
                    term = times(h_spec[s + 2, j], g)
                    part_acc[0, j] = term if s == 0 else part_acc[0, j] + term
                    add_corr(s + 2, j, g, r_next[j])

            if s == last_step:
                finish(j)
            return carry

        lax.fori_loop(0, chunks, step, 0)

    corr = halves(c_spec[...])
    both = jnp.concatenate(corr, axis=1)
    wide = dot(both, fwd_hi[...], TN)
    turned = wide[:lags] + wide[lags:] + dot(corr[0], fwd_lo[...], TN)
    below = jnp.concatenate([turned[nf:, :block], jnp.zeros((nf, block), jnp.float32)], axis=0)
    sums = (turned[:, block:] + below) * (1.0 / block)

    def c_copy(n, core):
        return remote(c_own.at[n, core], c_buf.at[z, c], c_send.at[n, core], c_recv.at[z, c], n * 2 + core)

    my_reach = jnp.where(z == chips - 2, chips - 1, jnp.where(z == chips - 1, 1, z))

    def reach(chip):
        return {chips - 2: chips - 1, chips - 1: 1}.get(chip, chip)

    for n in range(chips):
        c_own[n, 0] = sums[n * nf:(n + 1) * nf, :rows]
        c_own[n, 1] = sums[n * nf:(n + 1) * nf, rows:]

        @pl.when((n <= my_reach) & (n != z))
        def _():
            c_copy(n, 0).start()
            c_copy(n, 1).start()

    c_copy(z, 1 - c).start()

    def place(j, carry):
        for which, out, end in ((0, conv_ref, chips - 1), (1, gg_ref, 0)):
            y_copy(which, j).wait_recv()
            out[:, columns(1 - c, j)] = x_buf[which, j]

            @pl.when(z == end)
            def _():
                for core in range(2):
                    remote(part_buf.at[which, j, :rows, :], end_buf.at[which, core, j],
                           p_send.at[which, 0, j], p_recv.at[which, core, j], partner).wait_recv()
                    out[:, columns(core, j)] += end_buf[which, core, j]
        return carry

    lax.fori_loop(0, chunks, place, 0)

    def c_wait(chip, core):
        remote(c_own.at[0, 0], c_buf.at[chip, core], c_send.at[0, 0], c_recv.at[chip, core], partner).wait_recv()

    c_wait(z, 1 - c)
    gf_ref[pl.ds(pl.multiple_of(c * nf, nf), nf), :] = c_own[z, c]
    gf_ref[pl.ds(pl.multiple_of((1 - c) * nf, nf), nf), :] = c_buf[z, 1 - c]
    for i in range(1, chips):
        @pl.when((z <= reach(i)) & (i != z))
        def _():
            for core in range(2):
                c_wait(i, core)
                gf_ref[core * nf:(core + 1) * nf, :] += c_buf[i, core]

    c_copy(z, 1 - c).wait_send()
    for n in range(chips):
        @pl.when((n <= my_reach) & (n != z))
        def _():
            c_copy(n, 0).wait_send()
            c_copy(n, 1).wait_send()
    for d in range(1, groups):
        @pl.when(sends_filter(d))
        def _():
            filter_copy(d).wait_send()

    @pl.when(z == chips - 2)
    def _():
        filter_pass().wait_send()

    def drain(j, carry):
        for which in range(2):
            swap(which, j).wait_send()
            y_copy(which, j).wait_send()
        for which, sends in ((0, z + 1 < chips), (1, z >= 1)):
            @pl.when(sends)
            def _():
                own_copy(which, 0, j).wait_send()
                own_copy(which, 1, j).wait_send()

        for s in range(1, last_step + 1):
            @pl.when((z - s >= 0) & (z + 1 < chips - 1))
            def _():
                g_copy(s, j).wait_send()

            @pl.when((z + s < chips) & (z >= 2))
            def _():
                r_copy(s, j).wait_send()

        for which, near in ((0, chips - 2), (1, 1)):
            @pl.when(z == near)
            def _():
                part_copy(which, 0, j).wait_send()
                part_copy(which, 1, j).wait_send()
        return carry

    lax.fori_loop(0, chunks, drain, 0)


def scratch(chips, rows, half, nf):
    chunks, block = half // LANES, 2 * rows
    f32 = jnp.float32
    memory = [
        (chips, chunks, block, LANES),
        (chips, chunks, block, LANES),
        (2, chunks, rows, LANES),
        (chips, 2, nf, rows),
        (chips, chunks, 2 * block, LANES),
        (chunks, 2 * block, LANES),
        (chunks, 2 * block, LANES),
        (chunks, 2 * block, LANES),
        (chunks, 2 * block, LANES),
        (2, chunks, 2 * block, LANES),
        (2, chunks, block, LANES),
        (2 * block, chips * nf),
        (2, chunks, block, LANES),
        (2, chunks, rows, LANES),
        (chips, 2, nf, rows),
        (chips, 2, nf, rows),
        (2, 2, chunks, rows, LANES),
    ]
    steps = max(chips - 1, 1)
    sems = [
        (2 * chips,), (2 * chips,), (2, chunks), (2, chunks), (steps, chunks), (steps, chunks),
        (steps, chunks), (steps, chunks), (2, chunks), (2, chunks), (chips, 2), (chips, 2),
        (11,), (2, 2, chunks), (2, 2, chunks), (2, 2, chunks), (2, 2, chunks),
    ]
    used = sum(4 * math.prod(shape) for shape in memory)
    held = [((rows, 2 * half), jnp.bfloat16)] * 4 + [((2 * nf, rows), f32)]
    held += [((2 * block, 2 * block), jnp.bfloat16)] * 2 + [((block, 2 * block), jnp.bfloat16)] * 2
    held += [((chips, 2 * chips * nf, half), jnp.bfloat16), ((chips, chunks, 2 * LANES, chips * nf), jnp.bfloat16)]
    specs = [pltpu.VMEM(shape, kind) for shape, kind in held]
    specs += [pltpu.VMEM(shape, f32) for shape in memory]
    specs += [pltpu.SemaphoreType.DMA(shape) for shape in sems]
    return used, specs


def fits(chips, rows, width, filters):
    used, _ = scratch(chips, rows, width // 2, filters // 2)
    aligned = rows % LANES == 0 and chips * filters == 2 * LANES and width % (2 * LANES) == 0 and filters % 16 == 0
    return aligned and chips >= 3 and used <= VMEM_BUDGET // 2


def local_fast(query_gate, key_gate, value_in, filter_raw, grad_out):
    groups = lax.axis_size("context")
    chips = groups // 2
    rows, width = query_gate.shape
    filters = filter_raw.shape[1]
    half, nf, block = width // 2, filters // 2, 2 * rows
    chunks = half // LANES
    scale = 1.0 / math.sqrt(groups * rows)
    forward = tables(block)
    fwd = np_halves(forward)
    inv = np_halves(forward[:, block:].T / block)
    member = np.kron(np.eye(chips * nf), np.ones((1, width // filters)))
    member = member.reshape(chips * nf, chips, half).transpose(1, 0, 2)
    spread = np.tile(member, (1, 2, 1)).astype(jnp.bfloat16)
    gather = member.reshape(chips, chips * nf, chunks, LANES).transpose(0, 2, 3, 1)
    gather = np.tile(gather, (1, 1, 2, 1)).astype(jnp.bfloat16)
    _, scratches = scratch(chips, rows, half, nf)
    vmem = pl.BlockSpec(memory_space=pltpu.VMEM)
    conv, grad_gated, corr = pl.pallas_call(
        functools.partial(kernel, chips, scale),
        out_shape=(
            jax.ShapeDtypeStruct((rows, width), jnp.float32),
            jax.ShapeDtypeStruct((rows, width), jnp.float32),
            jax.ShapeDtypeStruct((filters, rows), jnp.float32),
        ),
        in_specs=[pl.BlockSpec(memory_space=pltpu.HBM)] * 11,
        out_specs=(vmem,) * 3,
        scratch_shapes=scratches,
        compiler_params=pltpu.CompilerParams(
            collective_id=0, has_side_effects=True, vmem_limit_bytes=VMEM_LIMIT),
        cost_estimate=pl.CostEstimate(flops=10**10, bytes_accessed=8 * 2**20, transcendentals=0),
        name="ring_conv",
    )(query_gate, key_gate, value_in, grad_out, filter_raw.T, *fwd, *inv, spread, gather)
    output = (query_gate.astype(jnp.float32) * conv).astype(jnp.bfloat16)
    grad_query = (grad_out.astype(jnp.float32) * conv).astype(jnp.bfloat16)
    grad_key = (grad_gated * value_in.astype(jnp.float32)).astype(jnp.bfloat16)
    grad_value = (grad_gated * key_gate.astype(jnp.float32)).astype(jnp.bfloat16)
    return output, grad_query, grad_key, grad_value, corr.T * scale


def dispatch(query_gate, key_gate, value_in, filter_raw, grad_out):
    args = (query_gate, key_gate, value_in, filter_raw, grad_out)
    rows, width = query_gate.shape
    if fits(lax.axis_size("context") // 2, rows, width, filter_raw.shape[1]):
        return local_fast(*args)
    return local(*args)


def solution(mesh):
    return jax.shard_map(
        dispatch,
        mesh=mesh,
        in_specs=(
            P("context", "tensor"),
            P("context", "tensor"),
            P("context", "tensor"),
            P("context", "tensor"),
            P("context", "tensor"),
        ),
        out_specs=(
            P("context", "tensor"),
            P("context", "tensor"),
            P("context", "tensor"),
            P("context", "tensor"),
            P("context", "tensor"),
        ),
        check_vma=False,
    )
```

```python
import functools
import math

import jax
import jax.numpy as jnp
import numpy as np
from jax import lax
from jax.experimental import pallas as pl
from jax.experimental.pallas import tpu as pltpu
from jax.sharding import PartitionSpec as P

highest = lax.Precision.HIGHEST


def phase_table(count_rows, count_cols, period):
    row_index = lax.broadcasted_iota(jnp.int32, (count_rows, count_cols), 0)
    col_index = lax.broadcasted_iota(jnp.int32, (count_rows, count_cols), 1)
    return (row_index * col_index % period).astype(jnp.float32) * (2.0 * math.pi / period)


def rotate(real_part, imag_part, cosine, sine):
    return (real_part * cosine - imag_part * sine, real_part * sine + imag_part * cosine)


def local(query_gate, key_gate, value_in, filter_raw, grad_out):
    groups = lax.axis_size("context")
    here = lax.axis_index("context")
    rows = query_gate.shape[0]
    width = query_gate.shape[1]
    filter_count = filter_raw.shape[1]
    group_size = width // filter_count
    points = 2 * groups * rows
    scale = 1.0 / math.sqrt(groups * rows)
    local_phase = phase_table(rows, rows, rows)
    cos_local = jnp.cos(local_phase)
    sin_local = jnp.sin(local_phase)
    row_iota = lax.broadcasted_iota(jnp.int32, (1, rows, 1), 1)
    parity = lax.broadcasted_iota(jnp.int32, (2, 1, 1), 0)

    def twiddle_phase(first):
        frequency = 2 * first + parity
        return (row_iota * frequency % points).astype(jnp.float32) * (2.0 * math.pi / points)

    def transpose_forward(signal):
        pieces = lax.all_to_all(signal[None], "context", split_axis=1, concat_axis=0, tiled=True)
        angles = phase_table(2 * groups, groups, 2 * groups)
        spread_re = jnp.einsum("ap,plc->alc", jnp.cos(angles), pieces, precision=highest)
        spread_im = -jnp.einsum("ap,plc->alc", jnp.sin(angles), pieces, precision=highest)
        return lax.all_to_all(
            jnp.stack([spread_re, spread_im]), "context", split_axis=1, concat_axis=2, tiled=True
        )

    def forward(signal):
        spec = transpose_forward(signal)
        phase = twiddle_phase(here)
        tw_re, tw_im = rotate(spec[0], spec[1], jnp.cos(phase), -jnp.sin(phase))
        out_re = jnp.einsum("br,erc->ebc", cos_local, tw_re, precision=highest) + jnp.einsum(
            "br,erc->ebc", sin_local, tw_im, precision=highest
        )
        out_im = jnp.einsum("br,erc->ebc", cos_local, tw_im, precision=highest) - jnp.einsum(
            "br,erc->ebc", sin_local, tw_re, precision=highest
        )
        return jnp.stack([out_re, out_im])

    def transpose_inverse(spec):
        pieces = lax.all_to_all(spec, "context", split_axis=2, concat_axis=1, tiled=True)
        angles = phase_table(groups, 2 * groups, 2 * groups)
        values = jnp.einsum(
            "pa,alc->plc", jnp.cos(angles), pieces[0], precision=highest
        ) - jnp.einsum("pa,alc->plc", jnp.sin(angles), pieces[1], precision=highest)
        return lax.all_to_all(values, "context", split_axis=0, concat_axis=1, tiled=True)[0]

    def turned(spec, first):
        loc_re = jnp.einsum("rb,ebc->erc", cos_local, spec[0], precision=highest) - jnp.einsum(
            "rb,ebc->erc", sin_local, spec[1], precision=highest
        )
        loc_im = jnp.einsum("rb,ebc->erc", cos_local, spec[1], precision=highest) + jnp.einsum(
            "rb,ebc->erc", sin_local, spec[0], precision=highest
        )
        phase = twiddle_phase(first)
        rot_re, rot_im = rotate(loc_re, loc_im, jnp.cos(phase), jnp.sin(phase))
        return jnp.stack([rot_re, rot_im])

    def inverse(spec):
        signal = transpose_inverse(turned(spec, here))
        return signal * (1.0 / points)

    def widen(part):
        spread = jnp.broadcast_to(part[..., None], part.shape + (group_size,))
        return spread.reshape(part.shape[:-1] + (width,))

    def group_total(part):
        return jnp.sum(part.reshape(part.shape[:-1] + (filter_count, group_size)), axis=-1)

    query_full = query_gate.astype(jnp.float32)
    key_full = key_gate.astype(jnp.float32)
    value_full = value_in.astype(jnp.float32)
    grad_full = grad_out.astype(jnp.float32)
    gated = key_full * value_full
    grad_conv = grad_full * query_full
    filt_part = filter_raw * scale
    spec_gated = forward(gated)
    spec_grad = forward(grad_conv)
    spec_filt = forward(filt_part)
    gated_re, gated_im = (spec_gated[0], spec_gated[1])
    filt_re, filt_im = (widen(spec_filt[0]), widen(spec_filt[1]))
    grad_re, grad_im = (spec_grad[0], spec_grad[1])
    conv_spec = jnp.stack(
        [gated_re * filt_re - gated_im * filt_im, gated_re * filt_im + gated_im * filt_re]
    )
    back_spec = jnp.stack(
        [filt_re * grad_re + filt_im * grad_im, filt_re * grad_im - filt_im * grad_re]
    )
    corr_spec = jnp.stack(
        [
            group_total(gated_re * grad_re + gated_im * grad_im),
            group_total(gated_re * grad_im - gated_im * grad_re),
        ]
    )
    conv = inverse(conv_spec)
    grad_gated = inverse(back_spec)
    corr = inverse(corr_spec)
    output = (query_full * conv).astype(jnp.bfloat16)
    grad_query = (grad_full * conv).astype(jnp.bfloat16)
    grad_key = (grad_gated * value_full).astype(jnp.bfloat16)
    grad_value = (grad_gated * key_full).astype(jnp.bfloat16)
    grad_filter = corr * scale
    return (output, grad_query, grad_key, grad_value, grad_filter)


LANES = 128
VMEM_BUDGET = 40 * 2**20
VMEM_LIMIT = 60 * 2**20


def halves(table):
    high = jnp.asarray(table, jnp.float32).astype(jnp.bfloat16)
    low = (jnp.asarray(table, jnp.float32) - high.astype(jnp.float32)).astype(jnp.bfloat16)
    return high, low


def np_halves(table):
    table = table.astype(np.float32)
    high = table.astype(jnp.bfloat16)
    low = (table - high.astype(np.float32)).astype(jnp.bfloat16)
    return high, low


def tables(block):
    k = np.arange(block, dtype=np.float64)[:, None] + 0.5
    n = np.arange(-block, block, dtype=np.float64)[None, :]
    angle = (np.pi / block) * k * n
    return np.concatenate([np.cos(angle), -np.sin(angle)], axis=0)


NN = (((1,), (0,)), ((), ()))
NT = (((1,), (1,)), ((), ()))
TN = (((0,), (0,)), ((), ()))


def dot(a, b, dims=NN):
    return lax.dot_general(a, b, dims, preferred_element_type=jnp.float32)


def dot3(a, b):
    count = b[0].shape[1]
    wide = dot(a[0], jnp.concatenate(b, axis=1))
    return wide[:, :count] + wide[:, count:] + dot(a[1], b[0])


def kernel(chips, scale, q_hbm, k_hbm, v_hbm, go_hbm, filt_hbm, fwd_hi_hbm, fwd_lo_hbm, inv_hi_hbm, inv_lo_hbm, spread_hbm, gather_hbm,
           conv_ref, gg_ref, gf_ref,
           q_ref, k_ref, v_ref, go_ref, filt_ref, fwd_hi, fwd_lo, inv_hi, inv_lo, spread_ref, gather_ref,
           g_buf, r_buf, sg_buf, h_buf, h_spec, conv_acc, gg_acc, r_spec, r_next, part_acc, part_buf, c_spec, y_buf, x_buf, c_own, c_buf, end_buf,
           f_send, f_recv, e_send, e_recv, g_send, g_recv, r_send, r_recv, y_send, y_recv, c_send, c_recv, load_sem, o_send, o_recv, p_send, p_recv):
    groups = 2 * chips
    rows = q_ref.shape[0]
    half = q_ref.shape[1] // 2
    block = 2 * rows
    chunks = half // LANES
    nf = filt_ref.shape[0] // 2
    me = lax.axis_index("context")
    z, c = me // 2, me % 2
    partner = z * 2 + (1 - c)
    right = (me + 2) % groups
    left = (me + groups - 2) % groups

    def remote(src, dst, send, recv, target):
        return pltpu.make_async_remote_copy(
            src_ref=src, dst_ref=dst, send_sem=send, recv_sem=recv,
            device_id={"context": target}, device_id_type=pl.DeviceIdType.MESH)

    def columns(which, j):
        return pl.ds(pl.multiple_of(which * half + j * LANES, LANES), LANES)

    my_rows = pl.ds(pl.multiple_of(c * rows, rows), rows)
    its_rows = pl.ds(pl.multiple_of((1 - c) * rows, rows), rows)

    loads = [pltpu.make_async_copy(src, dst, load_sem.at[i]) for i, (src, dst) in enumerate((
        (k_hbm, k_ref), (v_hbm, v_ref), (go_hbm, go_ref), (q_hbm, q_ref), (filt_hbm, filt_ref),
        (fwd_hi_hbm, fwd_hi), (fwd_lo_hbm, fwd_lo), (spread_hbm, spread_ref), (gather_hbm, gather_ref), (inv_hi_hbm, inv_hi),
        (inv_lo_hbm, inv_lo)))]
    for load in loads:
        load.start()

    barrier = pltpu.get_barrier_semaphore()
    for d in range(1, groups):
        pl.semaphore_signal(barrier, inc=1, device_id={"context": (me + d) % groups},
                            device_id_type=pl.DeviceIdType.MESH)
    def swap(which, j):
        buf = g_buf if which == 0 else r_buf
        return remote(sg_buf.at[which, j], buf.at[0, j, my_rows, :],
                      e_send.at[which, j], e_recv.at[which, j], partner)

    for load in loads[:5]:
        load.wait()

    def gate(j, carry):
        cols = columns(1 - c, j)
        sg_buf[0, j] = k_ref[:, cols].astype(jnp.float32) * v_ref[:, cols].astype(jnp.float32)
        sg_buf[1, j] = go_ref[:, cols].astype(jnp.float32) * q_ref[:, cols].astype(jnp.float32)
        cols = columns(c, j)
        g_buf[0, j, my_rows, :] = k_ref[:, cols].astype(jnp.float32) * v_ref[:, cols].astype(jnp.float32)
        r_buf[0, j, my_rows, :] = go_ref[:, cols].astype(jnp.float32) * q_ref[:, cols].astype(jnp.float32)
        return carry

    lax.fori_loop(0, chunks, gate, 0)
    pl.semaphore_wait(barrier, groups - 1)

    def filter_copy(d):
        target = (me + d) % groups
        part = pl.ds(pl.multiple_of((target % 2) * nf, nf), nf)
        return remote(filt_ref.at[part, :], h_buf.at[z, c], f_send.at[d], f_recv.at[d], target)

    def wanted(source, target):
        return (target <= chips - 2) & ((target >= 1) | (source <= 1))

    def sends_filter(d):
        return wanted(z, ((me + d) % groups) // 2)

    def gets_filter(d):
        return wanted(((me + groups - d) % groups) // 2, z)

    def filter_pass():
        return remote(h_buf.at[0:2], h_buf.at[0:2], f_send.at[0], f_recv.at[0], right)

    for d in range(1, groups):
        @pl.when(sends_filter(d))
        def _():
            filter_copy(d).start()

    @pl.when((z == 0) | (z == chips - 1))
    def _():
        h_buf[2:] = jnp.zeros((chips - 2, 2, nf, rows), jnp.float32)

    h_buf[z, c] = filt_ref[pl.ds(pl.multiple_of(c * nf, nf), nf), :]

    def own_copy(which, other, j):
        buf = g_buf if which == 0 else r_buf
        near = partner if other else me
        target = (near + 2) % groups if which == 0 else (near + groups - 2) % groups
        return remote(sg_buf.at[which, j] if other else buf.at[0, j, my_rows, :], buf.at[1, j, my_rows, :],
                      o_send.at[which, other, j], o_recv.at[which, c, j], target)

    def own_wait(which, j):
        buf = g_buf if which == 0 else r_buf
        for core in range(2):
            remote(sg_buf.at[which, j], buf.at[1, j, core * rows:(core + 1) * rows, :],
                   o_send.at[which, 0, j], o_recv.at[which, core, j], partner).wait_recv()

    def g_copy(s, j):
        return remote(g_buf.at[s, j], g_buf.at[s + 1, j], g_send.at[s, j], g_recv.at[s, j], right)

    def r_copy(s, j):
        return remote(r_buf.at[s, j], r_buf.at[s + 1, j], r_send.at[s, j], r_recv.at[s, j], left)

    def first_sends(j, carry):
        swap(0, j).start()
        swap(1, j).start()

        @pl.when(z + 1 < chips)
        def _():
            own_copy(0, 0, j).start()
            own_copy(0, 1, j).start()

        @pl.when(z >= 1)
        def _():
            own_copy(1, 0, j).start()
            own_copy(1, 1, j).start()
        return carry

    lax.fori_loop(0, chunks, first_sends, 0)

    for load in loads[5:]:
        load.wait()
    for d in range(1, groups):
        @pl.when(gets_filter(d))
        def _():
            filter_copy(d).wait_recv()

    @pl.when(z == chips - 2)
    def _():
        filter_pass().start()

    @pl.when(z == chips - 1)
    def _():
        filter_pass().wait_recv()

    lags = chips * nf
    taps = halves(jnp.concatenate(
        [h_buf[:, 0].reshape(lags, rows), h_buf[:, 1].reshape(lags, rows)], axis=1) * scale)
    wide = dot(fwd_hi[:, block:], jnp.concatenate(taps, axis=0), NT)
    spec = wide[:, :lags] + wide[:, lags:] + dot(fwd_lo[:, block:], taps[0], NT)
    early = jnp.concatenate([jnp.zeros((2 * block, nf), jnp.float32), spec[:, :lags - nf]], axis=1)
    sign = (1 - 2 * (lax.broadcasted_iota(jnp.int32, (block, lags), 0) % 2)).astype(jnp.float32)
    spec = jnp.concatenate(
        [spec[:block] - sign * early[block:], spec[block:] + sign * early[:block]], axis=0)
    spec = jnp.concatenate(halves(spec), axis=1)

    def widen(m, carry):
        full = dot(spec, spread_ref[m])
        for j in range(chunks):
            h_spec[m, j] = full[:, j * LANES:(j + 1) * LANES]
        return carry

    lax.fori_loop(0, chips, widen, 0)
    c_spec[...] = jnp.zeros_like(c_spec)

    def spectrum(signal):
        return dot3((fwd_hi[:, block:], fwd_lo[:, block:]), halves(signal))

    def conj_times(a, b):
        ar, ai, br, bi = a[:block], a[block:], b[:block], b[block:]
        return jnp.concatenate([ar * br + ai * bi, ar * bi - ai * br], axis=0)

    def times(a, b):
        ar, ai, br, bi = a[:block], a[block:], b[:block], b[block:]
        return jnp.concatenate([ar * br - ai * bi, ar * bi + ai * br], axis=0)

    def add_corr(m, j, g, r):
        prod = jnp.concatenate(halves(conj_times(g, r)), axis=1)
        c_spec[...] += dot(prod, gather_ref[m, j])

    def own_step(j, carry):
        swap(0, j).wait_recv()
        swap(1, j).wait_recv()
        r = spectrum(r_buf[0, j])
        r_spec[j] = r
        gg_acc[j] = conj_times(h_spec[0, j], r)
        g = spectrum(g_buf[0, j])
        conv_acc[j] = times(h_spec[0, j], g)
        add_corr(0, j, g, r)
        return carry

    lax.fori_loop(0, chunks, own_step, 0)

    def y_copy(which, j):
        return remote(y_buf.at[which, j, its_rows, :], x_buf.at[which, j],
                      y_send.at[which, j], y_recv.at[which, j], partner)

    def inverse(spec):
        return dot3((inv_hi[...], inv_lo[...]), halves(spec))

    def part_copy(which, core, j):
        chip = (z + 1 if which == 0 else z + chips - 1) % chips
        return remote(part_buf.at[which, j, core * rows:(core + 1) * rows, :], end_buf.at[which, c, j],
                      p_send.at[which, core, j], p_recv.at[which, c, j], chip * 2 + core)

    def add_part(which, s, j, term):
        total = term if s == 0 else part_acc[which, j] + term
        if s < last_step:
            part_acc[which, j] = total
        else:
            part_buf[which, j] = inverse(total)
            part_copy(which, 0, j).start()
            part_copy(which, 1, j).start()

    last_step = chips - 3

    def finish(j):
        for which, acc, out in ((0, conv_acc, conv_ref), (1, gg_acc, gg_ref)):
            y_buf[which, j] = inverse(acc[j])
            y_copy(which, j).start()
            out[:, columns(c, j)] = y_buf[which, j, my_rows, :]

    for s in range(last_step + 1):
        def step(j, carry):
            r_here = (z + 1 + s < chips) & ((z >= 1) | (s == 0))
            g_here = (z - 1 - s >= 0) & ((z <= chips - 2) | (s == 0))

            @pl.when(r_here)
            def _():
                own_wait(1, j) if s == 0 else r_copy(s, j).wait_recv()
                if s < last_step:
                    @pl.when(z >= 2)
                    def _():
                        r_copy(s + 1, j).start()

            @pl.when(g_here)
            def _():
                own_wait(0, j) if s == 0 else g_copy(s, j).wait_recv()
                if s < last_step:
                    @pl.when(z <= chips - 3)
                    def _():
                        g_copy(s + 1, j).start()

            @pl.when(r_here)
            def _():
                r = spectrum(r_buf[s + 1, j])

                @pl.when(z == 1)
                def _():
                    add_part(1, s, j, conj_times(h_spec[s + 2, j], r))

                gg_acc[j] += conj_times(h_spec[s + 1, j], r)
                if s == 0:
                    r_next[j] = r

            @pl.when(g_here)
            def _():
                g = spectrum(g_buf[s + 1, j])

                @pl.when(z == chips - 2)
                def _():
                    add_part(0, s, j, times(h_spec[s + 2, j], g))

                conv_acc[j] += times(h_spec[s + 1, j], g)
                add_corr(s + 1, j, g, r_spec[j])

                @pl.when(z == chips - 2)
                def _():
                    add_corr(s + 2, j, g, r_next[j])

            if s == last_step:
                finish(j)
            return carry

        lax.fori_loop(0, chunks, step, 0)

    corr = halves(c_spec[...])
    both = jnp.concatenate(corr, axis=1)
    wide = dot(both, fwd_hi[...], TN)
    turned = wide[:lags] + wide[lags:] + dot(corr[0], fwd_lo[...], TN)
    below = jnp.concatenate([turned[nf:, :block], jnp.zeros((nf, block), jnp.float32)], axis=0)
    sums = (turned[:, block:] + below) * (1.0 / block)

    def c_copy(n, core):
        return remote(c_own.at[n, core], c_buf.at[z, c], c_send.at[n, core], c_recv.at[z, c], n * 2 + core)

    my_reach = jnp.where(z == chips - 2, chips - 1, jnp.where(z == chips - 1, 1, z))

    def reach(chip):
        return {chips - 2: chips - 1, chips - 1: 1}.get(chip, chip)

    for n in range(chips):
        c_own[n, 0] = sums[n * nf:(n + 1) * nf, :rows]
        c_own[n, 1] = sums[n * nf:(n + 1) * nf, rows:]

        @pl.when((n <= my_reach) & (n != z))
        def _():
            c_copy(n, 0).start()
            c_copy(n, 1).start()

    c_copy(z, 1 - c).start()

    def place(j, carry):
        for which, out, end in ((0, conv_ref, chips - 1), (1, gg_ref, 0)):
            y_copy(which, j).wait_recv()
            out[:, columns(1 - c, j)] = x_buf[which, j]

            @pl.when(z == end)
            def _():
                for core in range(2):
                    remote(part_buf.at[which, j, :rows, :], end_buf.at[which, core, j],
                           p_send.at[which, 0, j], p_recv.at[which, core, j], partner).wait_recv()
                    out[:, columns(core, j)] += end_buf[which, core, j]
        return carry

    lax.fori_loop(0, chunks, place, 0)

    def c_wait(chip, core):
        remote(c_own.at[0, 0], c_buf.at[chip, core], c_send.at[0, 0], c_recv.at[chip, core], partner).wait_recv()

    c_wait(z, 1 - c)
    gf_ref[pl.ds(pl.multiple_of(c * nf, nf), nf), :] = c_own[z, c]
    gf_ref[pl.ds(pl.multiple_of((1 - c) * nf, nf), nf), :] = c_buf[z, 1 - c]
    for i in range(1, chips):
        @pl.when((z <= reach(i)) & (i != z))
        def _():
            for core in range(2):
                c_wait(i, core)
                gf_ref[core * nf:(core + 1) * nf, :] += c_buf[i, core]

    c_copy(z, 1 - c).wait_send()
    for n in range(chips):
        @pl.when((n <= my_reach) & (n != z))
        def _():
            c_copy(n, 0).wait_send()
            c_copy(n, 1).wait_send()
    for d in range(1, groups):
        @pl.when(sends_filter(d))
        def _():
            filter_copy(d).wait_send()

    @pl.when(z == chips - 2)
    def _():
        filter_pass().wait_send()

    def drain(j, carry):
        for which in range(2):
            swap(which, j).wait_send()
            y_copy(which, j).wait_send()
        for which, sends in ((0, z + 1 < chips), (1, z >= 1)):
            @pl.when(sends)
            def _():
                own_copy(which, 0, j).wait_send()
                own_copy(which, 1, j).wait_send()

        for s in range(1, last_step + 1):
            @pl.when((z - s >= 0) & (z + 1 < chips - 1))
            def _():
                g_copy(s, j).wait_send()

            @pl.when((z + s < chips) & (z >= 2))
            def _():
                r_copy(s, j).wait_send()

        for which, near in ((0, chips - 2), (1, 1)):
            @pl.when(z == near)
            def _():
                part_copy(which, 0, j).wait_send()
                part_copy(which, 1, j).wait_send()
        return carry

    lax.fori_loop(0, chunks, drain, 0)


def scratch(chips, rows, half, nf):
    chunks, block = half // LANES, 2 * rows
    f32 = jnp.float32
    memory = [
        (chips, chunks, block, LANES),
        (chips, chunks, block, LANES),
        (2, chunks, rows, LANES),
        (chips, 2, nf, rows),
        (chips, chunks, 2 * block, LANES),
        (chunks, 2 * block, LANES),
        (chunks, 2 * block, LANES),
        (chunks, 2 * block, LANES),
        (chunks, 2 * block, LANES),
        (2, chunks, 2 * block, LANES),
        (2, chunks, block, LANES),
        (2 * block, chips * nf),
        (2, chunks, block, LANES),
        (2, chunks, rows, LANES),
        (chips, 2, nf, rows),
        (chips, 2, nf, rows),
        (2, 2, chunks, rows, LANES),
    ]
    steps = max(chips - 1, 1)
    sems = [
        (2 * chips,), (2 * chips,), (2, chunks), (2, chunks), (steps, chunks), (steps, chunks),
        (steps, chunks), (steps, chunks), (2, chunks), (2, chunks), (chips, 2), (chips, 2),
        (11,), (2, 2, chunks), (2, 2, chunks), (2, 2, chunks), (2, 2, chunks),
    ]
    used = sum(4 * math.prod(shape) for shape in memory)
    held = [((rows, 2 * half), jnp.bfloat16)] * 4 + [((2 * nf, rows), f32)]
    held += [((2 * block, 2 * block), jnp.bfloat16)] * 2 + [((block, 2 * block), jnp.bfloat16)] * 2
    held += [((chips, 2 * chips * nf, half), jnp.bfloat16), ((chips, chunks, 2 * LANES, chips * nf), jnp.bfloat16)]
    specs = [pltpu.VMEM(shape, kind) for shape, kind in held]
    specs += [pltpu.VMEM(shape, f32) for shape in memory]
    specs += [pltpu.SemaphoreType.DMA(shape) for shape in sems]
    return used, specs


def fits(chips, rows, width, filters):
    used, _ = scratch(chips, rows, width // 2, filters // 2)
    aligned = rows % LANES == 0 and chips * filters == 2 * LANES and width % (2 * LANES) == 0 and filters % 16 == 0
    return aligned and chips >= 3 and used <= VMEM_BUDGET // 2


def local_fast(query_gate, key_gate, value_in, filter_raw, grad_out):
    groups = lax.axis_size("context")
    chips = groups // 2
    rows, width = query_gate.shape
    filters = filter_raw.shape[1]
    half, nf, block = width // 2, filters // 2, 2 * rows
    chunks = half // LANES
    scale = 1.0 / math.sqrt(groups * rows)
    forward = tables(block)
    fwd = np_halves(forward)
    inv = np_halves(forward[:, block:].T / block)
    member = np.kron(np.eye(chips * nf), np.ones((1, width // filters)))
    member = member.reshape(chips * nf, chips, half).transpose(1, 0, 2)
    spread = np.tile(member, (1, 2, 1)).astype(jnp.bfloat16)
    gather = member.reshape(chips, chips * nf, chunks, LANES).transpose(0, 2, 3, 1)
    gather = np.tile(gather, (1, 1, 2, 1)).astype(jnp.bfloat16)
    _, scratches = scratch(chips, rows, half, nf)
    vmem = pl.BlockSpec(memory_space=pltpu.VMEM)
    conv, grad_gated, corr = pl.pallas_call(
        functools.partial(kernel, chips, scale),
        out_shape=(
            jax.ShapeDtypeStruct((rows, width), jnp.float32),
            jax.ShapeDtypeStruct((rows, width), jnp.float32),
            jax.ShapeDtypeStruct((filters, rows), jnp.float32),
        ),
        in_specs=[pl.BlockSpec(memory_space=pltpu.HBM)] * 11,
        out_specs=(vmem,) * 3,
        scratch_shapes=scratches,
        compiler_params=pltpu.CompilerParams(
            collective_id=0, has_side_effects=True, vmem_limit_bytes=VMEM_LIMIT),
        cost_estimate=pl.CostEstimate(flops=10**10, bytes_accessed=8 * 2**20, transcendentals=0),
        name="ring_conv",
    )(query_gate, key_gate, value_in, grad_out, filter_raw.T, *fwd, *inv, spread, gather)
    output = (query_gate.astype(jnp.float32) * conv).astype(jnp.bfloat16)
    grad_query = (grad_out.astype(jnp.float32) * conv).astype(jnp.bfloat16)
    grad_key = (grad_gated * value_in.astype(jnp.float32)).astype(jnp.bfloat16)
    grad_value = (grad_gated * key_gate.astype(jnp.float32)).astype(jnp.bfloat16)
    return output, grad_query, grad_key, grad_value, corr.T * scale


def dispatch(query_gate, key_gate, value_in, filter_raw, grad_out):
    args = (query_gate, key_gate, value_in, filter_raw, grad_out)
    rows, width = query_gate.shape
    if fits(lax.axis_size("context") // 2, rows, width, filter_raw.shape[1]):
        return local_fast(*args)
    return local(*args)


def solution(mesh):
    return jax.shard_map(
        dispatch,
        mesh=mesh,
        in_specs=(
            P("context", "tensor"),
            P("context", "tensor"),
            P("context", "tensor"),
            P("context", "tensor"),
            P("context", "tensor"),
        ),
        out_specs=(
            P("context", "tensor"),
            P("context", "tensor"),
            P("context", "tensor"),
            P("context", "tensor"),
            P("context", "tensor"),
        ),
        check_vma=False,
    )
```

```python
import functools
import math

import jax
import jax.numpy as jnp
import numpy as np
from jax import lax
from jax.experimental import pallas as pl
from jax.experimental.pallas import tpu as pltpu
from jax.sharding import PartitionSpec as P

highest = lax.Precision.HIGHEST


def phase_table(count_rows, count_cols, period):
    row_index = lax.broadcasted_iota(jnp.int32, (count_rows, count_cols), 0)
    col_index = lax.broadcasted_iota(jnp.int32, (count_rows, count_cols), 1)
    return (row_index * col_index % period).astype(jnp.float32) * (2.0 * math.pi / period)


def rotate(real_part, imag_part, cosine, sine):
    return (real_part * cosine - imag_part * sine, real_part * sine + imag_part * cosine)


def local(query_gate, key_gate, value_in, filter_raw, grad_out):
    groups = lax.axis_size("context")
    here = lax.axis_index("context")
    rows = query_gate.shape[0]
    width = query_gate.shape[1]
    filter_count = filter_raw.shape[1]
    group_size = width // filter_count
    points = 2 * groups * rows
    scale = 1.0 / math.sqrt(groups * rows)
    local_phase = phase_table(rows, rows, rows)
    cos_local = jnp.cos(local_phase)
    sin_local = jnp.sin(local_phase)
    row_iota = lax.broadcasted_iota(jnp.int32, (1, rows, 1), 1)
    parity = lax.broadcasted_iota(jnp.int32, (2, 1, 1), 0)

    def twiddle_phase(first):
        frequency = 2 * first + parity
        return (row_iota * frequency % points).astype(jnp.float32) * (2.0 * math.pi / points)

    def transpose_forward(signal):
        pieces = lax.all_to_all(signal[None], "context", split_axis=1, concat_axis=0, tiled=True)
        angles = phase_table(2 * groups, groups, 2 * groups)
        spread_re = jnp.einsum("ap,plc->alc", jnp.cos(angles), pieces, precision=highest)
        spread_im = -jnp.einsum("ap,plc->alc", jnp.sin(angles), pieces, precision=highest)
        return lax.all_to_all(
            jnp.stack([spread_re, spread_im]), "context", split_axis=1, concat_axis=2, tiled=True
        )

    def forward(signal):
        spec = transpose_forward(signal)
        phase = twiddle_phase(here)
        tw_re, tw_im = rotate(spec[0], spec[1], jnp.cos(phase), -jnp.sin(phase))
        out_re = jnp.einsum("br,erc->ebc", cos_local, tw_re, precision=highest) + jnp.einsum(
            "br,erc->ebc", sin_local, tw_im, precision=highest
        )
        out_im = jnp.einsum("br,erc->ebc", cos_local, tw_im, precision=highest) - jnp.einsum(
            "br,erc->ebc", sin_local, tw_re, precision=highest
        )
        return jnp.stack([out_re, out_im])

    def transpose_inverse(spec):
        pieces = lax.all_to_all(spec, "context", split_axis=2, concat_axis=1, tiled=True)
        angles = phase_table(groups, 2 * groups, 2 * groups)
        values = jnp.einsum(
            "pa,alc->plc", jnp.cos(angles), pieces[0], precision=highest
        ) - jnp.einsum("pa,alc->plc", jnp.sin(angles), pieces[1], precision=highest)
        return lax.all_to_all(values, "context", split_axis=0, concat_axis=1, tiled=True)[0]

    def turned(spec, first):
        loc_re = jnp.einsum("rb,ebc->erc", cos_local, spec[0], precision=highest) - jnp.einsum(
            "rb,ebc->erc", sin_local, spec[1], precision=highest
        )
        loc_im = jnp.einsum("rb,ebc->erc", cos_local, spec[1], precision=highest) + jnp.einsum(
            "rb,ebc->erc", sin_local, spec[0], precision=highest
        )
        phase = twiddle_phase(first)
        rot_re, rot_im = rotate(loc_re, loc_im, jnp.cos(phase), jnp.sin(phase))
        return jnp.stack([rot_re, rot_im])

    def inverse(spec):
        signal = transpose_inverse(turned(spec, here))
        return signal * (1.0 / points)

    def widen(part):
        spread = jnp.broadcast_to(part[..., None], part.shape + (group_size,))
        return spread.reshape(part.shape[:-1] + (width,))

    def group_total(part):
        return jnp.sum(part.reshape(part.shape[:-1] + (filter_count, group_size)), axis=-1)

    query_full = query_gate.astype(jnp.float32)
    key_full = key_gate.astype(jnp.float32)
    value_full = value_in.astype(jnp.float32)
    grad_full = grad_out.astype(jnp.float32)
    gated = key_full * value_full
    grad_conv = grad_full * query_full
    filt_part = filter_raw * scale
    spec_gated = forward(gated)
    spec_grad = forward(grad_conv)
    spec_filt = forward(filt_part)
    gated_re, gated_im = (spec_gated[0], spec_gated[1])
    filt_re, filt_im = (widen(spec_filt[0]), widen(spec_filt[1]))
    grad_re, grad_im = (spec_grad[0], spec_grad[1])
    conv_spec = jnp.stack(
        [gated_re * filt_re - gated_im * filt_im, gated_re * filt_im + gated_im * filt_re]
    )
    back_spec = jnp.stack(
        [filt_re * grad_re + filt_im * grad_im, filt_re * grad_im - filt_im * grad_re]
    )
    corr_spec = jnp.stack(
        [
            group_total(gated_re * grad_re + gated_im * grad_im),
            group_total(gated_re * grad_im - gated_im * grad_re),
        ]
    )
    conv = inverse(conv_spec)
    grad_gated = inverse(back_spec)
    corr = inverse(corr_spec)
    output = (query_full * conv).astype(jnp.bfloat16)
    grad_query = (grad_full * conv).astype(jnp.bfloat16)
    grad_key = (grad_gated * value_full).astype(jnp.bfloat16)
    grad_value = (grad_gated * key_full).astype(jnp.bfloat16)
    grad_filter = corr * scale
    return (output, grad_query, grad_key, grad_value, grad_filter)


LANES = 128
VMEM_BUDGET = 40 * 2**20
VMEM_LIMIT = 60 * 2**20


def halves(table):
    high = jnp.asarray(table, jnp.float32).astype(jnp.bfloat16)
    low = (jnp.asarray(table, jnp.float32) - high.astype(jnp.float32)).astype(jnp.bfloat16)
    return high, low


def np_halves(table):
    table = table.astype(np.float32)
    high = table.astype(jnp.bfloat16)
    low = (table - high.astype(np.float32)).astype(jnp.bfloat16)
    return high, low


def tables(block):
    k = np.arange(block, dtype=np.float64)[:, None] + 0.5
    n = np.arange(-block, block, dtype=np.float64)[None, :]
    angle = (np.pi / block) * k * n
    return np.concatenate([np.cos(angle), -np.sin(angle)], axis=0)


NN = (((1,), (0,)), ((), ()))
NT = (((1,), (1,)), ((), ()))
TN = (((0,), (0,)), ((), ()))


def dot(a, b, dims=NN):
    return lax.dot_general(a, b, dims, preferred_element_type=jnp.float32)


def dot3(a, b):
    count = b[0].shape[1]
    wide = dot(a[0], jnp.concatenate(b, axis=1))
    return wide[:, :count] + wide[:, count:] + dot(a[1], b[0])


def kernel(chips, scale, q_hbm, k_hbm, v_hbm, go_hbm, filt_hbm, fwd_hi_hbm, fwd_lo_hbm, inv_hi_hbm, inv_lo_hbm, spread_hbm, gather_hbm,
           out_ref, gq_ref, gk_ref, gv_ref, gf_ref, conv_ref, gg_ref,
           q_ref, k_ref, v_ref, go_ref, filt_ref, fwd_hi, fwd_lo, inv_hi, inv_lo, spread_ref, gather_ref,
           g_buf, r_buf, sg_buf, h_buf, h_spec, conv_acc, gg_acc, r_spec, r_next, part_acc, part_buf, c_spec, y_buf, x_buf, c_own, c_buf, end_buf,
           f_send, f_recv, e_send, e_recv, g_send, g_recv, r_send, r_recv, y_send, y_recv, c_send, c_recv, load_sem, o_send, o_recv, p_send, p_recv):
    groups = 2 * chips
    rows = q_ref.shape[0]
    half = q_ref.shape[1] // 2
    block = 2 * rows
    chunks = half // LANES
    nf = filt_ref.shape[0] // 2
    me = lax.axis_index("context")
    z, c = me // 2, me % 2
    partner = z * 2 + (1 - c)
    right = (me + 2) % groups
    left = (me + groups - 2) % groups

    def remote(src, dst, send, recv, target):
        return pltpu.make_async_remote_copy(
            src_ref=src, dst_ref=dst, send_sem=send, recv_sem=recv,
            device_id={"context": target}, device_id_type=pl.DeviceIdType.MESH)

    def columns(which, j):
        return pl.ds(pl.multiple_of(which * half + j * LANES, LANES), LANES)

    my_rows = pl.ds(pl.multiple_of(c * rows, rows), rows)
    its_rows = pl.ds(pl.multiple_of((1 - c) * rows, rows), rows)

    loads = [pltpu.make_async_copy(src, dst, load_sem.at[i]) for i, (src, dst) in enumerate((
        (k_hbm, k_ref), (v_hbm, v_ref), (go_hbm, go_ref), (q_hbm, q_ref), (filt_hbm, filt_ref),
        (fwd_hi_hbm, fwd_hi), (fwd_lo_hbm, fwd_lo), (spread_hbm, spread_ref), (gather_hbm, gather_ref), (inv_hi_hbm, inv_hi),
        (inv_lo_hbm, inv_lo)))]
    for load in loads:
        load.start()

    barrier = pltpu.get_barrier_semaphore()
    for d in range(1, groups):
        pl.semaphore_signal(barrier, inc=1, device_id={"context": (me + d) % groups},
                            device_id_type=pl.DeviceIdType.MESH)
    def swap(which, j):
        buf = g_buf if which == 0 else r_buf
        return remote(sg_buf.at[which, j], buf.at[0, j, my_rows, :],
                      e_send.at[which, j], e_recv.at[which, j], partner)

    for load in loads[:5]:
        load.wait()

    def gate(j, carry):
        cols = columns(1 - c, j)
        sg_buf[0, j] = k_ref[:, cols].astype(jnp.float32) * v_ref[:, cols].astype(jnp.float32)
        sg_buf[1, j] = go_ref[:, cols].astype(jnp.float32) * q_ref[:, cols].astype(jnp.float32)
        cols = columns(c, j)
        g_buf[0, j, my_rows, :] = k_ref[:, cols].astype(jnp.float32) * v_ref[:, cols].astype(jnp.float32)
        r_buf[0, j, my_rows, :] = go_ref[:, cols].astype(jnp.float32) * q_ref[:, cols].astype(jnp.float32)
        return carry

    lax.fori_loop(0, chunks, gate, 0)
    pl.semaphore_wait(barrier, groups - 1)

    def filter_copy(d):
        target = (me + d) % groups
        part = pl.ds(pl.multiple_of((target % 2) * nf, nf), nf)
        return remote(filt_ref.at[part, :], h_buf.at[z, c], f_send.at[d], f_recv.at[d], target)

    def wanted(source, target):
        return (target <= chips - 2) & ((target >= 1) | (source <= 1))

    def sends_filter(d):
        return wanted(z, ((me + d) % groups) // 2)

    def gets_filter(d):
        return wanted(((me + groups - d) % groups) // 2, z)

    def filter_pass():
        return remote(h_buf.at[0:2], h_buf.at[0:2], f_send.at[0], f_recv.at[0], right)

    for d in range(1, groups):
        @pl.when(sends_filter(d))
        def _():
            filter_copy(d).start()

    @pl.when((z == 0) | (z == chips - 1))
    def _():
        h_buf[2:] = jnp.zeros((chips - 2, 2, nf, rows), jnp.float32)

    h_buf[z, c] = filt_ref[pl.ds(pl.multiple_of(c * nf, nf), nf), :]

    def own_copy(which, other, j):
        buf = g_buf if which == 0 else r_buf
        near = partner if other else me
        target = (near + 2) % groups if which == 0 else (near + groups - 2) % groups
        return remote(sg_buf.at[which, j] if other else buf.at[0, j, my_rows, :], buf.at[1, j, my_rows, :],
                      o_send.at[which, other, j], o_recv.at[which, c, j], target)

    def own_wait(which, j):
        buf = g_buf if which == 0 else r_buf
        for core in range(2):
            remote(sg_buf.at[which, j], buf.at[1, j, core * rows:(core + 1) * rows, :],
                   o_send.at[which, 0, j], o_recv.at[which, core, j], partner).wait_recv()

    def g_copy(s, j):
        return remote(g_buf.at[s, j], g_buf.at[s + 1, j], g_send.at[s, j], g_recv.at[s, j], right)

    def r_copy(s, j):
        return remote(r_buf.at[s, j], r_buf.at[s + 1, j], r_send.at[s, j], r_recv.at[s, j], left)

    def first_sends(j, carry):
        swap(0, j).start()
        swap(1, j).start()

        @pl.when(z + 1 < chips)
        def _():
            own_copy(0, 0, j).start()
            own_copy(0, 1, j).start()

        @pl.when(z >= 1)
        def _():
            own_copy(1, 0, j).start()
            own_copy(1, 1, j).start()
        return carry

    lax.fori_loop(0, chunks, first_sends, 0)

    for load in loads[5:]:
        load.wait()
    for d in range(1, groups):
        @pl.when(gets_filter(d))
        def _():
            filter_copy(d).wait_recv()

    @pl.when(z == chips - 2)
    def _():
        filter_pass().start()

    @pl.when(z == chips - 1)
    def _():
        filter_pass().wait_recv()

    lags = chips * nf
    taps = halves(jnp.concatenate(
        [h_buf[:, 0].reshape(lags, rows), h_buf[:, 1].reshape(lags, rows)], axis=1) * scale)
    wide = dot(fwd_hi[:, block:], jnp.concatenate(taps, axis=0), NT)
    spec = wide[:, :lags] + wide[:, lags:] + dot(fwd_lo[:, block:], taps[0], NT)
    early = jnp.concatenate([jnp.zeros((2 * block, nf), jnp.float32), spec[:, :lags - nf]], axis=1)
    sign = (1 - 2 * (lax.broadcasted_iota(jnp.int32, (block, lags), 0) % 2)).astype(jnp.float32)
    spec = jnp.concatenate(
        [spec[:block] - sign * early[block:], spec[block:] + sign * early[:block]], axis=0)
    spec = jnp.concatenate(halves(spec), axis=1)

    def widen(m, carry):
        full = dot(spec, spread_ref[m])
        for j in range(chunks):
            h_spec[m, j] = full[:, j * LANES:(j + 1) * LANES]
        return carry

    lax.fori_loop(0, chips, widen, 0)
    c_spec[...] = jnp.zeros_like(c_spec)

    def spectrum(signal):
        return dot3((fwd_hi[:, block:], fwd_lo[:, block:]), halves(signal))

    def conj_times(a, b):
        ar, ai, br, bi = a[:block], a[block:], b[:block], b[block:]
        return jnp.concatenate([ar * br + ai * bi, ar * bi - ai * br], axis=0)

    def times(a, b):
        ar, ai, br, bi = a[:block], a[block:], b[:block], b[block:]
        return jnp.concatenate([ar * br - ai * bi, ar * bi + ai * br], axis=0)

    def add_corr(m, j, g, r):
        prod = jnp.concatenate(halves(conj_times(g, r)), axis=1)
        c_spec[...] += dot(prod, gather_ref[m, j])

    def own_step(j, carry):
        swap(0, j).wait_recv()
        swap(1, j).wait_recv()
        r = spectrum(r_buf[0, j])
        r_spec[j] = r
        gg_acc[j] = conj_times(h_spec[0, j], r)
        g = spectrum(g_buf[0, j])
        conv_acc[j] = times(h_spec[0, j], g)
        add_corr(0, j, g, r)
        return carry

    lax.fori_loop(0, chunks, own_step, 0)

    def y_copy(which, j):
        return remote(y_buf.at[which, j, its_rows, :], x_buf.at[which, j],
                      y_send.at[which, j], y_recv.at[which, j], partner)

    def inverse(spec):
        return dot3((inv_hi[...], inv_lo[...]), halves(spec))

    def part_copy(which, core, j):
        chip = (z + 1 if which == 0 else z + chips - 1) % chips
        return remote(part_buf.at[which, j, core * rows:(core + 1) * rows, :], end_buf.at[which, c, j],
                      p_send.at[which, core, j], p_recv.at[which, c, j], chip * 2 + core)

    def add_part(which, s, j, term):
        total = term if s == 0 else part_acc[which, j] + term
        if s < last_step:
            part_acc[which, j] = total
        else:
            part_buf[which, j] = inverse(total)
            part_copy(which, 0, j).start()
            part_copy(which, 1, j).start()

    last_step = chips - 3

    def finish(j):
        for which, acc, out in ((0, conv_acc, conv_ref), (1, gg_acc, gg_ref)):
            y_buf[which, j] = inverse(acc[j])
            y_copy(which, j).start()
            out[:, columns(c, j)] = y_buf[which, j, my_rows, :]

    for s in range(last_step + 1):
        def step(j, carry):
            r_here = (z + 1 + s < chips) & ((z >= 1) | (s == 0))
            g_here = (z - 1 - s >= 0) & ((z <= chips - 2) | (s == 0))

            @pl.when(r_here)
            def _():
                own_wait(1, j) if s == 0 else r_copy(s, j).wait_recv()
                if s < last_step:
                    @pl.when(z >= 2)
                    def _():
                        r_copy(s + 1, j).start()

            @pl.when(g_here)
            def _():
                own_wait(0, j) if s == 0 else g_copy(s, j).wait_recv()
                if s < last_step:
                    @pl.when(z <= chips - 3)
                    def _():
                        g_copy(s + 1, j).start()

            @pl.when(r_here)
            def _():
                r = spectrum(r_buf[s + 1, j])

                @pl.when(z == 1)
                def _():
                    add_part(1, s, j, conj_times(h_spec[s + 2, j], r))

                gg_acc[j] += conj_times(h_spec[s + 1, j], r)
                if s == 0:
                    r_next[j] = r

            @pl.when(g_here)
            def _():
                g = spectrum(g_buf[s + 1, j])

                @pl.when(z == chips - 2)
                def _():
                    add_part(0, s, j, times(h_spec[s + 2, j], g))

                conv_acc[j] += times(h_spec[s + 1, j], g)
                add_corr(s + 1, j, g, r_spec[j])

                @pl.when(z == chips - 2)
                def _():
                    add_corr(s + 2, j, g, r_next[j])

            if s == last_step:
                finish(j)
            return carry

        lax.fori_loop(0, chunks, step, 0)

    corr = halves(c_spec[...])
    both = jnp.concatenate(corr, axis=1)
    wide = dot(both, fwd_hi[...], TN)
    turned = wide[:lags] + wide[lags:] + dot(corr[0], fwd_lo[...], TN)
    below = jnp.concatenate([turned[nf:, :block], jnp.zeros((nf, block), jnp.float32)], axis=0)
    sums = (turned[:, block:] + below) * (1.0 / block)

    def c_copy(n, core):
        return remote(c_own.at[n, core], c_buf.at[z, c], c_send.at[n, core], c_recv.at[z, c], n * 2 + core)

    my_reach = jnp.where(z == chips - 2, chips - 1, jnp.where(z == chips - 1, 1, z))

    def reach(chip):
        return {chips - 2: chips - 1, chips - 1: 1}.get(chip, chip)

    for n in range(chips):
        c_own[n, 0] = sums[n * nf:(n + 1) * nf, :rows]
        c_own[n, 1] = sums[n * nf:(n + 1) * nf, rows:]

        @pl.when((n <= my_reach) & (n != z))
        def _():
            c_copy(n, 0).start()
            c_copy(n, 1).start()

    c_copy(z, 1 - c).start()

    def place(j, carry):
        for which, out, end in ((0, conv_ref, chips - 1), (1, gg_ref, 0)):
            y_copy(which, j).wait_recv()
            out[:, columns(1 - c, j)] = x_buf[which, j]

            @pl.when(z == end)
            def _():
                for core in range(2):
                    remote(part_buf.at[which, j, :rows, :], end_buf.at[which, core, j],
                           p_send.at[which, 0, j], p_recv.at[which, core, j], partner).wait_recv()
                    out[:, columns(core, j)] += end_buf[which, core, j]

        for core in range(2):
            cols = columns(core, j)
            conv, grad = conv_ref[:, cols], gg_ref[:, cols]
            out_ref[:, cols] = (q_ref[:, cols].astype(jnp.float32) * conv).astype(jnp.bfloat16)
            gq_ref[:, cols] = (go_ref[:, cols].astype(jnp.float32) * conv).astype(jnp.bfloat16)
            gk_ref[:, cols] = (grad * v_ref[:, cols].astype(jnp.float32)).astype(jnp.bfloat16)
            gv_ref[:, cols] = (grad * k_ref[:, cols].astype(jnp.float32)).astype(jnp.bfloat16)
        return carry

    lax.fori_loop(0, chunks, place, 0)

    def c_wait(chip, core):
        remote(c_own.at[0, 0], c_buf.at[chip, core], c_send.at[0, 0], c_recv.at[chip, core], partner).wait_recv()

    c_wait(z, 1 - c)
    gf_ref[pl.ds(pl.multiple_of(c * nf, nf), nf), :] = c_own[z, c]
    gf_ref[pl.ds(pl.multiple_of((1 - c) * nf, nf), nf), :] = c_buf[z, 1 - c]
    for i in range(1, chips):
        @pl.when((z <= reach(i)) & (i != z))
        def _():
            for core in range(2):
                c_wait(i, core)
                gf_ref[core * nf:(core + 1) * nf, :] += c_buf[i, core]

    c_copy(z, 1 - c).wait_send()
    for n in range(chips):
        @pl.when((n <= my_reach) & (n != z))
        def _():
            c_copy(n, 0).wait_send()
            c_copy(n, 1).wait_send()
    for d in range(1, groups):
        @pl.when(sends_filter(d))
        def _():
            filter_copy(d).wait_send()

    @pl.when(z == chips - 2)
    def _():
        filter_pass().wait_send()

    def drain(j, carry):
        for which in range(2):
            swap(which, j).wait_send()
            y_copy(which, j).wait_send()
        for which, sends in ((0, z + 1 < chips), (1, z >= 1)):
            @pl.when(sends)
            def _():
                own_copy(which, 0, j).wait_send()
                own_copy(which, 1, j).wait_send()

        for s in range(1, last_step + 1):
            @pl.when((z - s >= 0) & (z + 1 < chips - 1))
            def _():
                g_copy(s, j).wait_send()

            @pl.when((z + s < chips) & (z >= 2))
            def _():
                r_copy(s, j).wait_send()

        for which, near in ((0, chips - 2), (1, 1)):
            @pl.when(z == near)
            def _():
                part_copy(which, 0, j).wait_send()
                part_copy(which, 1, j).wait_send()
        return carry

    lax.fori_loop(0, chunks, drain, 0)


def scratch(chips, rows, half, nf):
    chunks, block = half // LANES, 2 * rows
    f32 = jnp.float32
    memory = [
        (chips, chunks, block, LANES),
        (chips, chunks, block, LANES),
        (2, chunks, rows, LANES),
        (chips, 2, nf, rows),
        (chips, chunks, 2 * block, LANES),
        (chunks, 2 * block, LANES),
        (chunks, 2 * block, LANES),
        (chunks, 2 * block, LANES),
        (chunks, 2 * block, LANES),
        (2, chunks, 2 * block, LANES),
        (2, chunks, block, LANES),
        (2 * block, chips * nf),
        (2, chunks, block, LANES),
        (2, chunks, rows, LANES),
        (chips, 2, nf, rows),
        (chips, 2, nf, rows),
        (2, 2, chunks, rows, LANES),
    ]
    steps = max(chips - 1, 1)
    sems = [
        (2 * chips,), (2 * chips,), (2, chunks), (2, chunks), (steps, chunks), (steps, chunks),
        (steps, chunks), (steps, chunks), (2, chunks), (2, chunks), (chips, 2), (chips, 2),
        (11,), (2, 2, chunks), (2, 2, chunks), (2, 2, chunks), (2, 2, chunks),
    ]
    used = sum(4 * math.prod(shape) for shape in memory)
    held = [((rows, 2 * half), f32)] * 2 + [((rows, 2 * half), jnp.bfloat16)] * 4 + [((2 * nf, rows), f32)]
    held += [((2 * block, 2 * block), jnp.bfloat16)] * 2 + [((block, 2 * block), jnp.bfloat16)] * 2
    held += [((chips, 2 * chips * nf, half), jnp.bfloat16), ((chips, chunks, 2 * LANES, chips * nf), jnp.bfloat16)]
    specs = [pltpu.VMEM(shape, kind) for shape, kind in held]
    specs += [pltpu.VMEM(shape, f32) for shape in memory]
    specs += [pltpu.SemaphoreType.DMA(shape) for shape in sems]
    return used, specs


def fits(chips, rows, width, filters):
    used, _ = scratch(chips, rows, width // 2, filters // 2)
    aligned = rows % LANES == 0 and chips * filters == 2 * LANES and width % (2 * LANES) == 0 and filters % 16 == 0
    return aligned and chips >= 3 and used <= VMEM_BUDGET // 2


def local_fast(query_gate, key_gate, value_in, filter_raw, grad_out):
    groups = lax.axis_size("context")
    chips = groups // 2
    rows, width = query_gate.shape
    filters = filter_raw.shape[1]
    half, nf, block = width // 2, filters // 2, 2 * rows
    chunks = half // LANES
    scale = 1.0 / math.sqrt(groups * rows)
    forward = tables(block)
    fwd = np_halves(forward)
    inv = np_halves(forward[:, block:].T / block)
    member = np.kron(np.eye(chips * nf), np.ones((1, width // filters)))
    member = member.reshape(chips * nf, chips, half).transpose(1, 0, 2)
    spread = np.tile(member, (1, 2, 1)).astype(jnp.bfloat16)
    gather = member.reshape(chips, chips * nf, chunks, LANES).transpose(0, 2, 3, 1)
    gather = np.tile(gather, (1, 1, 2, 1)).astype(jnp.bfloat16)
    _, scratches = scratch(chips, rows, half, nf)
    vmem = pl.BlockSpec(memory_space=pltpu.VMEM)
    *gates, corr = pl.pallas_call(
        functools.partial(kernel, chips, scale),
        out_shape=(
            *[jax.ShapeDtypeStruct((rows, width), jnp.bfloat16)] * 4,
            jax.ShapeDtypeStruct((filters, rows), jnp.float32),
        ),
        in_specs=[pl.BlockSpec(memory_space=pltpu.HBM)] * 11,
        out_specs=(vmem,) * 5,
        scratch_shapes=scratches,
        compiler_params=pltpu.CompilerParams(
            collective_id=0, has_side_effects=True, vmem_limit_bytes=VMEM_LIMIT),
        cost_estimate=pl.CostEstimate(flops=10**10, bytes_accessed=8 * 2**20, transcendentals=0),
        name="ring_conv",
    )(query_gate, key_gate, value_in, grad_out, filter_raw.T, *fwd, *inv, spread, gather)
    return *gates, corr.T * scale


def dispatch(query_gate, key_gate, value_in, filter_raw, grad_out):
    args = (query_gate, key_gate, value_in, filter_raw, grad_out)
    rows, width = query_gate.shape
    if fits(lax.axis_size("context") // 2, rows, width, filter_raw.shape[1]):
        return local_fast(*args)
    return local(*args)


def solution(mesh):
    return jax.shard_map(
        dispatch,
        mesh=mesh,
        in_specs=(
            P("context", "tensor"),
            P("context", "tensor"),
            P("context", "tensor"),
            P("context", "tensor"),
            P("context", "tensor"),
        ),
        out_specs=(
            P("context", "tensor"),
            P("context", "tensor"),
            P("context", "tensor"),
            P("context", "tensor"),
            P("context", "tensor"),
        ),
        check_vma=False,
    )
```
